256 devices in a mesh: tm: 32 (over z, y), feat: 8 (over x, core).
Axes of the slice: x: 4, y: 4, z: 8, core: 2. Of those that a mesh axis runs over, the one named last changes fastest.
Arguments:
- tile_data: bfloat16 [2048, 32, 128, 128], P('tm', 'feat'), may hold values from -1 to 1
- tile_ids: int32 [2048, 32], P('tm', 'feat'), may hold values from 0 to 31, as said below
- owner_perm: int32 [2048], P('tm'), may hold values from 0 to 2047, as said below
- events: int32 [2048, 128], P('tm'), may hold values 0 or 1
- groups: int32 [2048, 128], P('tm'), may hold values from 0 to 127, as said below
- coefficients: bfloat16 [32768], P('feat'), may hold values from -4 to 4
Outputs:
- gradient: float32 [32768], P('feat')
- newton_step: float32 [32768], P('feat')
The draws below stay inside these ranges and needn't reach their ends.
Inputs may be any that keep to these rules, and one draw needn't show every extreme that they name: `tile_ids`: in each feature shard's 4 columns a row block names 4 different local feature blocks. `owner_perm`: A permutation of row blocks; each patient shard of 64 row blocks sends exactly 2 of them to each time shard. `groups`: group numbers start at 0 in every row block and never fall within it; a tied group never spans two row blocks.
All inputs are finite; a program needn't handle non-finite values. No bound on the sum of `events` on one device may be relied on, other than what follows from the above.
Results may differ from the reference program's by a relative error of at most 0.00035.
The reference program's roundings to bfloat16 on the way count: a program that leaves them out, or rounds other values in their place, can miss the bound.
Values may be sent and summed in bfloat16 or wider, within the bound.
A program may use at most 128 MiB of HBM per device.

```python
import math
import jax
import jax.numpy as jnp
from jax import lax

TILE = 128
FBD = 32
K = 4
CAP = 2
RB = 64
NRB = 2048
KS = 32
FEATS = 32768
N_FEAT = 8


def draw_tile_data(key, part):
    window = 8
    spread_factor = 1.0 / math.sqrt(window * TILE * KS)
    block_keys = jax.random.split(jax.random.fold_in(key, 7), NRB)

    def one_block(block_key):
        noise_field = jnp.clip(jax.random.normal(block_key, (KS, TILE, TILE + window - 1), jnp.float32), -3.0, 3.0)
        summed = noise_field[:, :, 0:TILE]
        for offset in range(1, window):
            summed = summed + noise_field[:, :, offset:offset + TILE]
        return (summed * spread_factor).astype(jnp.bfloat16)
    return lax.map(one_block, block_keys)


def draw_tile_ids(key, part):
    shard_count = KS // K
    random_bits = jax.random.randint(jax.random.fold_in(key, 3), (NRB, shard_count, FBD), 0, 2 ** 30)
    sorting = jnp.argsort(random_bits, axis=-1, stable=True)
    return sorting[:, :, :K].reshape(NRB, KS).astype(jnp.int32)


def draw_owner_perm(key, part):
    shard_count = RB // CAP
    first_key = jax.random.fold_in(key, 11)
    second_key = jax.random.fold_in(key, 13)
    source_perm = jax.vmap(lambda k: jax.random.permutation(k, RB))(jax.random.split(first_key, shard_count))
    target = source_perm // CAP
    within = source_perm % CAP
    target_perm = jax.vmap(lambda k: jax.random.permutation(k, RB))(jax.random.split(second_key, shard_count))
    source_index = jnp.arange(shard_count, dtype=jnp.int32)[:, None]
    arrival_slot = target_perm[target, source_index * CAP + within]
    return (target * RB + arrival_slot).reshape(NRB).astype(jnp.int32)


def draw_groups(key, part):
    starts = jax.random.randint(jax.random.fold_in(key, 5), (NRB, TILE), 0, 2)
    starts = starts.at[0, :].set(1)
    starts = starts.at[:, 0].set(0)
    return jnp.cumsum(starts, axis=1).astype(jnp.int32)


def set_ends(drawn, own_key, smallest, largest):
    dims = drawn.shape
    place = [jax.random.randint(jax.random.fold_in(own_key, axis), (), 0, dims[axis]) for axis in range(len(dims))]
    drawn = drawn.at[tuple(place)].set(smallest)
    longest = dims.index(max(dims))
    place[longest] = (place[longest] + 1) % dims[longest]
    return drawn.at[tuple(place)].set(largest)


def shard_levels(key, extent, cuts, low, high):
    factor_of, own = 1.0, jax.random.fold_in(key, 6)
    for position, blocks in cuts:
        draws = jnp.exp(jax.random.uniform(jax.random.fold_in(own, position), (blocks,), jnp.float32, low / len(cuts), high / len(cuts)))
        factor_of = factor_of * jnp.repeat(draws, extent[position] // blocks).reshape([-1 if axis == position else 1 for axis in range(len(extent))])
    return factor_of


def scatter_about(key, extent, width, limit, pieces=(), kind=jnp.bfloat16):
    drawn = jax.random.normal(key, extent, jnp.float32) * width
    if len(pieces) > 0:
        drawn = shard_levels(key, extent, pieces, -0.22, 0.18) * drawn
    return jnp.clip(drawn, min=-limit, max=limit).astype(kind)


def setup_inputs(seed: int = 0) -> dict:
    key_of = jax.random.split(jax.random.key(seed), 7)
    return {
        "tile_data": draw_tile_data(jax.random.fold_in(key_of[6], 71), 0),
        "tile_ids": draw_tile_ids(jax.random.fold_in(key_of[6], 71), 0),
        "owner_perm": draw_owner_perm(jax.random.fold_in(key_of[6], 71), 0),
        "events": set_ends((jax.random.randint(key_of[3], (NRB, TILE), 0, 2) < 1).astype(jnp.int32), jax.random.fold_in(key_of[3], 1), 0, 1),
        "groups": draw_groups(jax.random.fold_in(key_of[6], 71), 0),
        "coefficients": scatter_about(key_of[5], (FEATS,), 1.0, 4.0, ((0, 8),)),
    }


ridge_weight = 1.0

def reference(tile_data, tile_ids, owner_perm, events, groups, coefficients):
    blocks = coefficients.reshape(FBD * N_FEAT, TILE)
    shard_of = (jnp.arange(KS) // K).astype(jnp.int32)
    block_ids = (tile_ids + shard_of[None, :] * FBD).astype(jnp.int32)

    def block_eta(element):
        tile_set, chosen = element
        picked = blocks[chosen].astype(jnp.float32)
        return jnp.einsum('spt,st->p', tile_set.astype(jnp.float32), picked, precision=lax.Precision.HIGHEST)
    cohort_eta = lax.map(block_eta, (tile_data, block_ids))
    time_eta = jnp.zeros((NRB, TILE), jnp.float32).at[owner_perm].set(cohort_eta)
    event_flag = jnp.zeros((NRB, TILE), jnp.float32).at[owner_perm].set(events.astype(jnp.float32))
    risk_score = jnp.exp(time_eta)
    later_mask = (groups[:, None, :] >= groups[:, :, None]).astype(jnp.float32)
    later_in = jnp.einsum('bik,bk->bi', later_mask, risk_score, precision=lax.Precision.HIGHEST)
    block_tot = jnp.sum(risk_score, axis=1)
    after_blocks = jnp.concatenate([jnp.cumsum(block_tot[::-1])[::-1][1:], jnp.zeros((1,), jnp.float32)])
    risk_total = after_blocks[:, None] + later_in
    hazard_one = event_flag / risk_total
    hazard_two = hazard_one / risk_total
    earlier_one = jnp.einsum('bki,bk->bi', later_mask, hazard_one, precision=lax.Precision.HIGHEST)
    earlier_two = jnp.einsum('bki,bk->bi', later_mask, hazard_two, precision=lax.Precision.HIGHEST)
    tot_one = jnp.sum(hazard_one, axis=1)
    tot_two = jnp.sum(hazard_two, axis=1)
    before_one = jnp.concatenate([jnp.zeros((1,), jnp.float32), jnp.cumsum(tot_one)[:-1]])
    before_two = jnp.concatenate([jnp.zeros((1,), jnp.float32), jnp.cumsum(tot_two)[:-1]])
    cum_one = before_one[:, None] + earlier_one
    cum_two = before_two[:, None] + earlier_two
    residual = event_flag - risk_score * cum_one
    weight = risk_score * cum_one - risk_score * risk_score * cum_two
    resid_cohort = residual[owner_perm]
    weight_cohort = weight[owner_perm]

    def accumulate(totals, element):
        grad_sum, hess_sum = totals
        tile_set, chosen, resid_row, weight_row = element
        as_float = tile_set.astype(jnp.float32)
        resid_round = lax.optimization_barrier(resid_row.astype(jnp.bfloat16)).astype(jnp.float32)
        weighted = lax.optimization_barrier((as_float * weight_row[None, :, None]).astype(jnp.bfloat16)).astype(jnp.float32)
        grad_slots = jnp.einsum('spa,p->sa', as_float, resid_round, precision=lax.Precision.HIGHEST)
        hess_slots = jnp.einsum('spa,spb->sab', weighted, as_float, precision=lax.Precision.HIGHEST)
        return ((grad_sum.at[chosen].add(grad_slots), hess_sum.at[chosen].add(hess_slots)), None)
    start = (jnp.zeros((FBD * N_FEAT, TILE), jnp.float32), jnp.zeros((FBD * N_FEAT, TILE, TILE), jnp.float32))
    (gradient, hessian), unused = lax.scan(accumulate, start, (tile_data, block_ids, resid_cohort, weight_cohort))
    system = hessian + ridge_weight * jnp.eye(TILE, dtype=jnp.float32)[None]
    factor = jnp.linalg.cholesky(system)
    newton_step = jax.scipy.linalg.cho_solve((factor, True), gradient[:, :, None])[:, :, 0]
    return (gradient.reshape(FEATS), newton_step.reshape(FEATS))
```

```python
import functools
import math

import jax
import jax.numpy as jnp
from jax import lax
from jax.experimental import pallas as pl
from jax.experimental.pallas import tpu as pltpu
from jax.sharding import PartitionSpec as P

MESH = pl.DeviceIdType.MESH
TILE = 128
HALF = 64
PACK = 72
SHIFTS = (1, 2, 4, 8, 16, 32, 64)
Y_SIZE = 4
CHUNKS = 4


def lanes_of(rows):
    return lax.broadcasted_iota(jnp.int32, (rows, TILE), 1)


def scores_kernel(
    n_tm, n_feat,
    tiles, ids, perm_row, events, groups, coef,
    resid_out, weight_out,
    held, eta_parts, perm_all, group_send, group_recv, sum_one, sum_two, pay_one, pay_two, shifted,
    tile_sem, eta_send, eta_recv, perm_send, perm_recv, grp_send, grp_recv,
    one_send, one_recv, two_send, two_recv,
):
    me = lax.axis_index("tm")
    mf = lax.axis_index("feat")
    rows = events.shape[0]
    per = rows // CHUNKS
    slots = tiles.shape[1]

    def tile_copy(q):
        part = pl.ds(q * per, per)
        return pltpu.make_async_copy(tiles.at[part], held.at[part], tile_sem.at[q])

    for q in range(CHUNKS):
        tile_copy(q).start()

    barrier = pltpu.get_barrier_semaphore()

    def greet_tm(i, c):
        pl.semaphore_signal(
            barrier, inc=1, device_id=(lax.rem(me + i, n_tm), mf), device_id_type=MESH
        )
        return c

    def greet_feat(i, c):
        pl.semaphore_signal(
            barrier, inc=1, device_id=(me, lax.rem(mf + i, n_feat)), device_id_type=MESH
        )
        return c

    lax.fori_loop(1, n_tm, greet_tm, 0)
    lax.fori_loop(1, n_feat, greet_feat, 0)
    pl.semaphore_wait(barrier, n_tm + n_feat - 2)

    def tm_send(src_of, dst, send_sem, recv_sem):
        def one(i, c):
            peer = lax.rem(me + i, n_tm)
            pltpu.make_async_remote_copy(
                src_ref=src_of(peer), dst_ref=dst.at[me],
                send_sem=send_sem.at[peer], recv_sem=recv_sem.at[me],
                device_id=(peer, mf), device_id_type=MESH,
            ).start()
            return c

        lax.fori_loop(1, n_tm, one, 0)

    def tm_wait(src_of, dst, send_sem, recv_sem):
        def one(i, c):
            peer = lax.rem(me + i, n_tm)
            copy = pltpu.make_async_remote_copy(
                src_ref=src_of(peer), dst_ref=dst.at[peer],
                send_sem=send_sem.at[peer], recv_sem=recv_sem.at[peer],
                device_id=(peer, mf), device_id_type=MESH,
            )
            copy.wait_recv()
            copy.wait_send()
            return c

        lax.fori_loop(1, n_tm, one, 0)

    perm_all[me] = perm_row[...]
    tm_send(lambda peer: perm_row, perm_all, perm_send, perm_recv)

    chunk_lane = lanes_of(TILE)

    def eta_copy(q, peer, slot):
        part = pl.ds(q * per, per)
        return pltpu.make_async_remote_copy(
            src_ref=eta_parts.at[mf, part], dst_ref=eta_parts.at[slot, part],
            send_sem=eta_send.at[q, peer], recv_sem=eta_recv.at[q, slot],
            device_id=(me, peer), device_id_type=MESH,
        )

    def eta_chunk(q):
        tile_copy(q).wait()

        def one(i, kept):
            n = q * per + i
            total = held[n, 0].astype(jnp.float32) * coef[ids[n, 0]]
            for s in range(1, slots):
                total = total + held[n, s].astype(jnp.float32) * coef[ids[n, s]]
            column = jnp.sum(total, axis=1, keepdims=True)
            return jnp.where(chunk_lane == i, column, kept)

        columns = lax.fori_loop(0, per, one, jnp.zeros((TILE, TILE), jnp.float32))
        eta_parts[mf, q * per : (q + 1) * per, :] = columns.T[:per, :]

        def send(i, c):
            eta_copy(q, lax.rem(mf + i, n_feat), mf).start()
            return c

        lax.fori_loop(1, n_feat, send, 0)

    lane = lanes_of(rows)
    row = lax.broadcasted_iota(jnp.int32, (rows, TILE), 0)
    diagonal = lane == row
    perm_col = jnp.sum(
        jnp.where(diagonal, perm_row[...], 0.0), axis=1, keepdims=True
    )

    eta_chunk(0)

    tm_wait(lambda peer: perm_row, perm_all, perm_send, perm_recv)
    every = perm_all[:, 0, :]
    shard = jnp.floor(every * (1.0 / rows))
    within = every - shard * rows
    mine = jnp.logical_and(shard == me.astype(jnp.float32), lanes_of(n_tm) < rows)
    low = jnp.min(jnp.where(mine, within, 4096.0), axis=1, keepdims=True)
    high = jnp.max(jnp.where(mine, within, -1.0), axis=1, keepdims=True)
    place = lax.broadcasted_iota(jnp.int32, (n_tm, rows), 1).astype(jnp.float32)
    group_bf = groups[...].astype(jnp.float32).astype(jnp.bfloat16)
    first = jnp.dot(
        jnp.where(place == low, 1.0, 0.0).astype(jnp.bfloat16), group_bf,
        preferred_element_type=jnp.float32,
    )
    second = jnp.dot(
        jnp.where(place == high, 1.0, 0.0).astype(jnp.bfloat16), group_bf,
        preferred_element_type=jnp.float32,
    )
    for c in range(n_tm):
        group_send[c, :, 0:TILE] = first[c : c + 1, :]
        group_send[c, :, TILE : 2 * TILE] = second[c : c + 1, :]
    group_recv[me] = group_send[me]
    tm_send(lambda peer: group_send.at[peer], group_recv, grp_send, grp_recv)

    for q in range(1, CHUNKS):
        eta_chunk(q)

    tm_wait(lambda peer: group_send.at[peer], group_recv, grp_send, grp_recv)
    my_shard = jnp.floor(perm_col * (1.0 / rows))
    same = jnp.logical_and(
        jnp.floor(perm_row[...] * (1.0 / rows)) == my_shard, perm_row[...] < perm_col
    )
    rank = jnp.sum(
        jnp.where(jnp.logical_and(same, lane < rows), 1.0, 0.0), axis=1, keepdims=True
    )
    shard_lane = lax.broadcasted_iota(jnp.int32, (rows, n_tm), 1).astype(jnp.float32)
    hit = jnp.where(shard_lane == my_shard, 1.0, 0.0)
    cohort_groups = jnp.dot(
        (hit * (1.0 - rank)).astype(jnp.bfloat16),
        group_recv[:, 0, 0:TILE].astype(jnp.bfloat16),
        preferred_element_type=jnp.float32,
    ) + jnp.dot(
        (hit * rank).astype(jnp.bfloat16),
        group_recv[:, 0, TILE : 2 * TILE].astype(jnp.bfloat16),
        preferred_element_type=jnp.float32,
    )
    for k, d in enumerate(SHIFTS):
        back = pltpu.roll(cohort_groups, d, 1)
        shifted[k] = jnp.where(jnp.logical_and(lane >= d, back == cohort_groups), 1.0, 0.0)
        ahead = pltpu.roll(cohort_groups, TILE - d, 1)
        shifted[len(SHIFTS) + k] = jnp.where(
            jnp.logical_and(lane < TILE - d, ahead == cohort_groups), 1.0, 0.0
        )
    event_flag = events[...].astype(jnp.float32)

    for q in range(CHUNKS):
        def wait(i, c, q=q):
            peer = lax.rem(mf + i, n_feat)
            copy = eta_copy(q, peer, peer)
            copy.wait_recv()
            copy.wait_send()
            return c

        lax.fori_loop(1, n_feat, wait, 0)
    eta = eta_parts[0]
    for f in range(1, n_feat):
        eta = eta + eta_parts[f]
    risk = jnp.exp(eta)

    suffix = risk
    for d in SHIFTS:
        suffix = suffix + jnp.where(lane < TILE - d, pltpu.roll(suffix, TILE - d, 1), 0.0)
    pay_one[...] = jnp.sum(
        jnp.where(diagonal, suffix[:, 0:1], 0.0), axis=0, keepdims=True
    )
    sum_one[me] = pay_one[...]
    tm_send(lambda peer: pay_one, sum_one, one_send, one_recv)
    later = suffix
    for k, d in enumerate(SHIFTS):
        later = jnp.where(shifted[k] > 0.5, pltpu.roll(later, d, 1), later)
    tm_wait(lambda peer: pay_one, sum_one, one_send, one_recv)

    def add_later(c, total):
        return total + jnp.where(perm_all[c] > perm_col, sum_one[c], 0.0)

    after = lax.fori_loop(0, n_tm, add_later, jnp.zeros((rows, TILE), jnp.float32))
    risk_total = later + jnp.sum(after, axis=1, keepdims=True)
    hazard_one = event_flag / risk_total
    hazard_two = hazard_one / risk_total
    prefix_one, prefix_two = hazard_one, hazard_two
    for d in SHIFTS:
        prefix_one = prefix_one + jnp.where(lane >= d, pltpu.roll(prefix_one, d, 1), 0.0)
        prefix_two = prefix_two + jnp.where(lane >= d, pltpu.roll(prefix_two, d, 1), 0.0)
    pay_two[...] = jnp.sum(
        jnp.where(diagonal, prefix_one[:, TILE - 1 : TILE], 0.0)
        + jnp.where(lane == row + HALF, prefix_two[:, TILE - 1 : TILE], 0.0),
        axis=0, keepdims=True,
    )
    sum_two[me] = pay_two[...]
    tm_send(lambda peer: pay_two, sum_two, two_send, two_recv)
    early_one, early_two = prefix_one, prefix_two
    for k, d in enumerate(SHIFTS):
        tied = shifted[len(SHIFTS) + k] > 0.5
        early_one = jnp.where(tied, pltpu.roll(early_one, TILE - d, 1), early_one)
        early_two = jnp.where(tied, pltpu.roll(early_two, TILE - d, 1), early_two)
    tm_wait(lambda peer: pay_two, sum_two, two_send, two_recv)

    def add_early(c, total):
        return total + jnp.where(perm_all[c] < perm_col, sum_two[c], 0.0)

    before = lax.fori_loop(0, n_tm, add_early, jnp.zeros((rows, TILE), jnp.float32))
    cum_one = early_one + jnp.sum(
        jnp.where(lane < HALF, before, 0.0), axis=1, keepdims=True
    )
    cum_two = early_two + jnp.sum(
        jnp.where(lane < HALF, 0.0, before), axis=1, keepdims=True
    )
    resid_out[...] = event_flag - risk * cum_one
    weight_out[...] = risk * cum_one - risk * risk * cum_two


def gram_kernel(tiles, ids, resid, weight, total):
    step = pl.program_id(0)
    rows, slots = tiles.shape[:2]

    @pl.when(step == 0)
    def _():
        total[...] = jnp.zeros_like(total)

    for n in range(rows):
        scale = weight[n : n + 1, :]
        rounded = jnp.broadcast_to(resid[n : n + 1, :], (16, TILE)).astype(jnp.bfloat16)
        for s in range(slots):
            tile = tiles[n, s]
            turned = (tile.T.astype(jnp.float32) * scale).astype(jnp.bfloat16)
            block = ids[step * rows + n, s]
            total[block] += jnp.dot(
                jnp.concatenate([turned, rounded], axis=0), tile,
                preferred_element_type=jnp.float32,
            )


def eliminate(system, rhs):
    tiles = TILE // 8
    sub = lax.broadcasted_iota(jnp.int32, (8, TILE), 0)
    a = tuple(system[8 * i : 8 * i + 8, :] for i in range(tiles))
    g = tuple(rhs[8 * i : 8 * i + 8, :] for i in range(tiles))

    def spread(x, r):
        return jnp.broadcast_to(x[r : r + 1, :], (8, TILE))

    def panel(p, carry):
        a, g = list(carry[0]), list(carry[1])
        cols = [
            [jnp.broadcast_to(a[i][:, r : r + 1], (8, TILE)) for i in range(tiles)]
            for r in range(8)
        ]
        for r in range(8):
            inverse = 1.0 / spread(cols[r][0], r)
            factor = [c * inverse for c in cols[r]]
            factor[0] = jnp.where(sub == r, 1.0 - inverse, factor[0])
            for later in range(r + 1, 8):
                pivot = spread(cols[later][0], r)
                for i in range(tiles):
                    cols[later][i] = cols[later][i] - factor[i] * pivot
            pivot_a, pivot_g = spread(a[0], r), spread(g[0], r)
            for i in range(tiles):
                a[i] = a[i] - factor[i] * pivot_a
                g[i] = g[i] - factor[i] * pivot_g
        a = [pltpu.roll(x, TILE - 8, 1) for x in a]
        return tuple(a[1:] + a[:1]), tuple(g[1:] + g[:1])

    _, g = lax.fori_loop(0, tiles, panel, (a, g))
    return jnp.concatenate(g, axis=0)


def solve_kernel(
    n_z, n_y,
    parts, grad_out, step_out,
    packed, first, middle, second, grad_row, step_row,
    first_send, first_recv, second_send, second_recv, grad_send, grad_recv, step_send, step_recv,
):
    n_tm = n_z * n_y
    me = lax.axis_index("tm")
    mf = lax.axis_index("feat")
    z = lax.div(me, n_y)
    y = lax.rem(me, n_y)
    barrier = pltpu.get_barrier_semaphore()

    def greet(i, c):
        pl.semaphore_signal(
            barrier, inc=1, device_id=(lax.rem(me + i, n_tm), mf), device_id_type=MESH
        )
        return c

    lax.fori_loop(1, n_tm, greet, 0)
    pl.semaphore_wait(barrier, n_tm - 1)

    lane8 = lanes_of(8)
    sub8 = lax.broadcasted_iota(jnp.int32, (8, TILE), 0)

    def pack(block, to):
        whole = parts[block, 0:TILE, :]
        whole = 0.5 * (whole + whole.T)
        for i in range(7):
            width = 120 - 8 * i
            low = whole[8 * (14 - i) : 8 * (14 - i) + 8, :]
            high = pltpu.roll(whole[8 * i : 8 * i + 8, :], width, 1)
            to[8 * i : 8 * i + 8, :] = jnp.where(lane8 < width, low, high)
        grad = parts[block, TILE : TILE + 8, :]
        tail = jnp.where(sub8 == 0, grad, pltpu.roll(grad, HALF, 1))
        to[56:64, :] = jnp.where(lane8 < HALF, whole[56:64, :], tail)
        to[64:72, :] = whole[120:128, :]

    half_z = n_z // 2

    def far(k):
        return half_z + jnp.where(lax.rem(k, 2) == 1, -lax.div(k + 1, 2), lax.div(k, 2))

    def first_copy(k, dy):
        return pltpu.make_async_remote_copy(
            src_ref=packed.at[dy, k], dst_ref=first.at[dy - 1, k],
            send_sem=first_send.at[dy - 1, k], recv_sem=first_recv.at[dy - 1, k],
            device_id=(z * n_y + lax.rem(y + dy, n_y), mf), device_id_type=MESH,
        )

    def second_copy(k):
        return pltpu.make_async_remote_copy(
            src_ref=middle.at[k], dst_ref=second.at[k],
            send_sem=second_send.at[k], recv_sem=second_recv.at[k],
            device_id=(lax.rem(z + far(k), n_z) * n_y + y, mf), device_id_type=MESH,
        )

    def send_first(k, c):
        to_z = lax.rem(z + far(k), n_z)
        for dy in list(range(1, n_y)) + [0]:
            pack(to_z * n_y + lax.rem(y + dy, n_y), packed.at[dy, k])
            if dy:
                first_copy(k, dy).start()
        return c

    lax.fori_loop(0, n_z, send_first, 0)

    def gathered(k):
        for dy in range(1, n_y):
            first_copy(k, dy).wait_recv()
        total = packed[0, k]
        for dy in range(1, n_y):
            total = total + first[dy - 1, k]
        return total

    def send_second(k, c):
        middle[k] = gathered(k)
        second_copy(k).start()
        return c

    lax.fori_loop(0, n_z - 1, send_second, 0)
    total = gathered(n_z - 1)
    for k in range(n_z - 1):
        second_copy(k).wait_recv()
        total = total + second[k]

    pieces = [total[8 * i : 8 * i + 8, :] for i in range(9)]
    turned = pltpu.roll(pieces[7], HALF, 1)
    gradient = jnp.where(lane8[0:1] < HALF, turned[1:2, :], pieces[7][0:1, :])
    grad_row[...] = gradient
    grad_out[me] = gradient

    def gather_copy(i, src, dst, send_sem, recv_sem, incoming):
        peer = lax.rem(me + i, n_tm)
        at = peer if incoming else me
        return pltpu.make_async_remote_copy(
            src_ref=src, dst_ref=dst.at[at], send_sem=send_sem.at[peer], recv_sem=recv_sem.at[at],
            device_id=(peer, mf), device_id_type=MESH,
        )

    def send_grad(i, c):
        gather_copy(i, grad_row, grad_out, grad_send, grad_recv, False).start()
        return c

    lax.fori_loop(1, n_tm, send_grad, 0)

    tile_rows = [pltpu.roll(pieces[i], 8 + 8 * i, 1) for i in range(7)]
    tile_rows += [pieces[7]] + [pieces[14 - i] for i in range(8, 15)] + [pieces[8]]
    stacked = jnp.concatenate(tile_rows, axis=0)
    row = lax.broadcasted_iota(jnp.int32, (TILE, TILE), 0)
    lane = lanes_of(TILE)
    lower = jnp.where(lane <= row, stacked, 0.0)
    upper = jnp.where(lane < row, stacked, 0.0).T
    system = lower + upper + jnp.where(lane == row, 1.0, 0.0)
    column = jnp.sum(jnp.where(lane == row, gradient, 0.0), axis=1, keepdims=True)
    solved = eliminate(system, jnp.broadcast_to(column, (TILE, TILE)))
    answer = jnp.sum(jnp.where(lane == row, solved, 0.0), axis=0, keepdims=True)
    step_row[...] = answer
    step_out[me] = answer

    def send_step(i, c):
        gather_copy(i, step_row, step_out, step_send, step_recv, False).start()
        return c

    lax.fori_loop(1, n_tm, send_step, 0)
    for k in range(n_z):
        for dy in range(1, n_y):
            first_copy(k, dy).wait_send()
        if k < n_z - 1:
            second_copy(k).wait_send()

    def finish(i, c):
        for copy in (
            gather_copy(i, grad_row, grad_out, grad_send, grad_recv, True),
            gather_copy(i, step_row, step_out, step_send, step_recv, True),
        ):
            copy.wait_recv()
            copy.wait_send()
        return c

    lax.fori_loop(1, n_tm, finish, 0)


def local(tile_data, tile_ids, owner_perm, events, groups, coefficients):
    rows, slots = tile_data.shape[:2]
    n_tm, n_feat = lax.axis_size("tm"), lax.axis_size("feat")
    n_y = min(Y_SIZE, n_tm // 2)
    n_z = n_tm // n_y
    blocks = coefficients.shape[0] // TILE
    f32, vmem = jnp.float32, pl.BlockSpec(memory_space=pltpu.VMEM)
    smem, anywhere = pl.BlockSpec(memory_space=pltpu.SMEM), pl.BlockSpec(memory_space=pl.ANY)
    dma = pltpu.SemaphoreType.DMA
    coef = coefficients.astype(f32).reshape(blocks, 1, TILE)
    perm = owner_perm.astype(f32)
    perm = jnp.pad(perm, (0, HALF - rows))
    perm_row = jnp.concatenate([perm, perm]).reshape(1, TILE)

    resid, weight = pl.pallas_call(
        functools.partial(scores_kernel, n_tm, n_feat),
        out_shape=[jax.ShapeDtypeStruct((rows, TILE), f32)] * 2,
        in_specs=[anywhere, smem, vmem, vmem, vmem, vmem],
        out_specs=[vmem, vmem],
        scratch_shapes=[
            pltpu.VMEM(tile_data.shape, jnp.bfloat16),
            pltpu.VMEM((n_feat, rows, TILE), f32),
            pltpu.VMEM((n_tm, 1, TILE), f32),
            pltpu.VMEM((n_tm, 1, 2 * TILE), f32),
            pltpu.VMEM((n_tm, 1, 2 * TILE), f32),
            pltpu.VMEM((n_tm, 1, TILE), f32),
            pltpu.VMEM((n_tm, 1, TILE), f32),
            pltpu.VMEM((1, TILE), f32),
            pltpu.VMEM((1, TILE), f32),
            pltpu.VMEM((2 * len(SHIFTS), rows, TILE), f32),
            dma((CHUNKS,)),
            dma((CHUNKS, n_feat)), dma((CHUNKS, n_feat)),
            dma((n_tm,)), dma((n_tm,)), dma((n_tm,)), dma((n_tm,)),
            dma((n_tm,)), dma((n_tm,)), dma((n_tm,)), dma((n_tm,)),
        ],
        compiler_params=pltpu.CompilerParams(
            collective_id=0, has_side_effects=True, vmem_limit_bytes=40 * 2**20
        ),
        name="scores",
    )(tile_data, tile_ids, perm_row, events, groups, coef)

    group = 8
    parts = pl.pallas_call(
        gram_kernel,
        out_shape=jax.ShapeDtypeStruct((blocks, TILE + 16, TILE), f32),
        grid=(rows // group,),
        in_specs=[
            pl.BlockSpec((group, slots, TILE, TILE), lambda i: (i, 0, 0, 0)),
            smem,
            pl.BlockSpec((group, TILE), lambda i: (i, 0)),
            pl.BlockSpec((group, TILE), lambda i: (i, 0)),
        ],
        out_specs=pl.BlockSpec((blocks, TILE + 16, TILE), lambda i: (0, 0, 0)),
        compiler_params=pltpu.CompilerParams(vmem_limit_bytes=40 * 2**20),
        name="gram",
    )(tile_data, tile_ids, resid, weight)

    gradient, step = pl.pallas_call(
        functools.partial(solve_kernel, n_z, n_y),
        out_shape=[jax.ShapeDtypeStruct((n_tm, 1, TILE), f32)] * 2,
        in_specs=[vmem],
        out_specs=[vmem, vmem],
        scratch_shapes=[
            pltpu.VMEM((n_y, n_z, PACK, TILE), f32),
            pltpu.VMEM((n_y - 1, n_z, PACK, TILE), f32),
            pltpu.VMEM((n_z, PACK, TILE), f32),
            pltpu.VMEM((n_z, PACK, TILE), f32),
            pltpu.VMEM((1, TILE), f32),
            pltpu.VMEM((1, TILE), f32),
            dma((n_y - 1, n_z)), dma((n_y - 1, n_z)), dma((n_z,)), dma((n_z,)),
            dma((n_tm,)), dma((n_tm,)), dma((n_tm,)), dma((n_tm,)),
        ],
        compiler_params=pltpu.CompilerParams(
            collective_id=1, has_side_effects=True, vmem_limit_bytes=40 * 2**20
        ),
        name="solve",
    )(parts)
    return gradient.reshape(-1), step.reshape(-1)


def solution(mesh):
    return jax.shard_map(
        local,
        mesh=mesh,
        in_specs=(
            P("tm", "feat", None, None),
            P("tm", "feat"),
            P("tm"),
            P("tm", None),
            P("tm", None),
            P("feat"),
        ),
        out_specs=(P("feat"), P("feat")),
        check_vma=False,
    )
```

```python
import functools

import jax
import jax.numpy as jnp
from jax import lax
from jax.experimental import pallas as pl
from jax.experimental.pallas import tpu as pltpu
from jax.sharding import PartitionSpec as P

MESH = pl.DeviceIdType.MESH
TILE = 128
HALF = 64
PACK = 72
SHIFTS = (1, 2, 4, 8, 16, 32, 64)
Y_SIZE = 4
CHUNKS = 4
CUT = 40
UNROLL = 18


def lanes_of(rows):
    return lax.broadcasted_iota(jnp.int32, (rows, TILE), 1)


def three_parts(x):
    high = x.astype(jnp.bfloat16)
    rest = x - high.astype(jnp.float32)
    mid = rest.astype(jnp.bfloat16)
    low = (rest - mid.astype(jnp.float32)).astype(jnp.bfloat16)
    return high, mid, low


def times_ones(x, mask):
    rows = x.shape[0]
    out = jnp.dot(
        jnp.concatenate(three_parts(x), axis=0),
        jnp.where(mask, 1.0, 0.0).astype(jnp.bfloat16),
        preferred_element_type=jnp.float32,
    )
    return out[2 * rows :] + out[rows : 2 * rows] + out[:rows]


def eliminate(system, rhs, wide=32):
    tiles = wide // 8
    sub = lax.broadcasted_iota(jnp.int32, (8, TILE), 0)

    def spread(x, r):
        return jnp.broadcast_to(x[r : r + 1, :], (8, TILE))

    def panel(p, carry):
        whole, right = carry
        a = [whole[8 * i : 8 * i + 8, :] for i in range(tiles)]
        g = [right[8 * i : 8 * i + 8, :] for i in range(tiles)]
        for q in range(tiles):
            cols = [
                [
                    jnp.broadcast_to(a[i][:, 8 * q + r : 8 * q + r + 1], (8, TILE))
                    for i in range(tiles)
                ]
                for r in range(8)
            ]
            head = [cols[r][q] for r in range(8)]
            top, top_g = a[q], g[q]
            for r in range(8):
                inverse = 1.0 / spread(head[r], r)
                factor = jnp.where(sub == r, 1.0 - inverse, head[r] * inverse)
                for k in range(r + 1, 8):
                    head[k] = head[k] - factor * spread(head[k], r)
                top = top - factor * spread(top, r)
                top_g = top_g - factor * spread(top_g, r)
            for i in range(tiles):
                if i != q:
                    for r in range(8):
                        a[i] = a[i] - cols[r][i] * spread(top, r)
                        g[i] = g[i] - cols[r][i] * spread(top_g, r)
            a[q], g[q] = top, top_g
        done, done_g = jnp.concatenate(a, axis=0), jnp.concatenate(g, axis=0)
        rest = whole[wide:, :]
        update = jnp.dot(
            rest[:, :wide], jnp.concatenate([done, done_g], axis=1),
            precision=lax.Precision.HIGHEST, preferred_element_type=jnp.float32,
        )
        whole = jnp.concatenate([rest - update[:, :TILE], done], axis=0)
        right = jnp.concatenate([right[wide:, :] - update[:, TILE:], done_g], axis=0)
        return pltpu.roll(whole, TILE - wide, 1), right

    return lax.fori_loop(0, TILE // wide, panel, (system, rhs))[1]


def newton_kernel(
    n_z, n_y, n_feat,
    tiles, ids, id_rows, perm, events, groups, coef,
    grad_out, step_out,
    held, event_buf, group_buf, perm_buf, id_buf, coef_buf, coef_wide, eta_rows,
    eta_parts, perm_all, group_send, group_recv, sum_one, sum_two,
    table_buf, table, weight_rows, resid_rows, running,
    packed, chain, ring, middle, second, grad_row, step_row,
    tile_sem, small_sem, table_sem, eta_send, eta_recv, perm_send, perm_recv, grp_send, grp_recv,
    one_send, one_recv, two_send, two_recv,
    chain_send, chain_recv, ring_send, ring_recv, second_send, second_recv,
    grad_send, grad_recv, step_send, step_recv,
):
    n_tm = n_z * n_y
    z = lax.div(lax.axis_index("tm"), n_y)
    y = lax.rem(lax.axis_index("tm"), n_y)
    me = lax.axis_index("tm")
    mf = lax.axis_index("feat")
    rows = events.shape[0]
    per = rows // CHUNKS
    slots, blocks = id_rows.shape[0], coef.shape[0]
    count = rows * slots
    barrier = pltpu.get_barrier_semaphore()

    def greet_tm(i, c):
        pl.semaphore_signal(
            barrier, inc=1, device_id=(lax.rem(me + i, n_tm), mf), device_id_type=MESH
        )
        return c

    def greet_feat(i, c):
        pl.semaphore_signal(
            barrier, inc=1, device_id=(me, lax.rem(mf + i, n_feat)), device_id_type=MESH
        )
        return c

    def tile_copy(q):
        part = pl.ds(q * per * slots, per * slots)
        return pltpu.make_async_copy(tiles.at[part], held.at[part], tile_sem.at[q])

    small = [
        pltpu.make_async_copy(source, target, small_sem.at[k])
        for k, (source, target) in enumerate(
            ((coef, coef_buf), (perm, perm_buf), (groups, group_buf), (events, event_buf), (id_rows, id_buf))
        )
    ]
    small[0].start()
    tile_copy(0).start()
    lax.fori_loop(1, n_tm, greet_tm, 0)
    lax.fori_loop(1, n_feat, greet_feat, 0)
    for q in range(1, CHUNKS):
        tile_copy(q).start()
    for copy in small[1:]:
        copy.start()

    def tm_copy(i, source, target, send_sem, recv_sem, sign):
        peer = lax.rem(me + sign * i + n_tm, n_tm)
        return pltpu.make_async_remote_copy(
            src_ref=source(i), dst_ref=target.at[i],
            send_sem=send_sem.at[i], recv_sem=recv_sem.at[i],
            device_id=(peer, mf), device_id_type=MESH,
        )

    def tm_send(*how):
        def one(i, c):
            tm_copy(i, *how).start()
            return c

        lax.fori_loop(1, n_tm, one, 0)

    def tm_wait(*how):
        def one(i, c):
            copy = tm_copy(i, *how)
            copy.wait_recv()
            copy.wait_send()
            return c

        lax.fori_loop(1, n_tm, one, 0)

    small[0].wait()
    wide = coef_buf[...].astype(jnp.float32)
    for j in range(blocks):
        coef_wide[j] = wide[j : j + 1, :]

    def eta_copy(q, i):
        part = pl.ds(q * per, per)
        return pltpu.make_async_remote_copy(
            src_ref=eta_parts.at[0, part], dst_ref=eta_parts.at[i, part],
            send_sem=eta_send.at[q, i], recv_sem=eta_recv.at[q, i],
            device_id=(me, lax.rem(mf + i, n_feat)), device_id_type=MESH,
        )

    def eta_make(q):
        tile_copy(q).wait()
        together = min(4, per)

        def some(k, c):
            for u in range(together):
                i = k * together + u
                n = q * per + i
                total = None
                for s in range(slots):
                    term = held[n * slots + s].astype(jnp.float32) * coef_wide[ids[s, n]]
                    total = term if total is None else total + term
                eta_rows[i] = jnp.sum(total.T, axis=0, keepdims=True)
            return c

        lax.fori_loop(0, per // together, some, 0)
        eta_parts[0, q * per : (q + 1) * per, :] = jnp.concatenate(
            [eta_rows[i] for i in range(per)], axis=0
        )

    def eta_start(q):
        for i in range(1, n_feat):
            eta_copy(q, i).start()

    lane = lanes_of(rows)
    row = lax.broadcasted_iota(jnp.int32, (rows, TILE), 0)
    diagonal = lane == row
    for q in range(CHUNKS - 1):
        eta_make(q)
    small[1].wait()
    gap = jnp.zeros((1, HALF - rows), jnp.int32)
    perm_all[0] = jnp.concatenate(
        [perm_buf[...], gap] * 2 if rows < HALF else [perm_buf[...]] * 2, axis=1
    )
    pl.semaphore_wait(barrier, n_tm + n_feat - 2)
    perm_how = (lambda i: perm_all.at[0], perm_all, perm_send, perm_recv, 1)
    tm_send(*perm_how)
    for q in range(CHUNKS - 1):
        eta_start(q)
    eta_make(CHUNKS - 1)
    eta_start(CHUNKS - 1)

    held[count] = jnp.zeros((TILE, TILE), jnp.bfloat16)
    resid_rows[rows] = jnp.zeros((1, TILE), jnp.float32)
    weight_rows[rows] = jnp.zeros((1, TILE), jnp.float32)
    running[running.shape[0] - 1] = jnp.zeros(running.shape[1:], jnp.float32)
    table_buf[...] = jnp.zeros_like(table_buf)

    for copy in small[2:]:
        copy.wait()
    event_flag = event_buf[...].astype(jnp.float32)
    group_bf = group_buf[...].astype(jnp.float32).astype(jnp.bfloat16)
    place = lax.broadcasted_iota(jnp.int32, (n_tm, rows), 1).astype(jnp.float32)
    perm_row = perm_all[0].astype(jnp.float32)
    perm_col = jnp.sum(jnp.where(diagonal, perm_row, 0.0), axis=1, keepdims=True)
    my_shard = jnp.floor(perm_col * (1.0 / rows))
    same = jnp.logical_and(jnp.floor(perm_row * (1.0 / rows)) == my_shard, perm_row < perm_col)
    rank = jnp.sum(
        jnp.where(jnp.logical_and(same, lane < rows), 1.0, 0.0), axis=1, keepdims=True
    )
    id_all = id_buf[...]
    block_at = lax.broadcasted_iota(jnp.int32, (blocks, rows), 0)
    row_at = lax.broadcasted_iota(jnp.int32, (blocks, rows), 1)
    present = jnp.zeros((blocks, rows), jnp.float32)
    which = jnp.zeros((blocks, rows), jnp.float32)
    for s in range(slots):
        here = id_all[s : s + 1, :] == block_at
        present = present + jnp.where(here, 1.0, 0.0)
        which = which + jnp.where(here, (row_at * slots + s).astype(jnp.float32), 0.0)
    before_row = jnp.where(
        lax.broadcasted_iota(jnp.int32, (rows, rows), 0)
        < lax.broadcasted_iota(jnp.int32, (rows, rows), 1), 1.0, 0.0,
    ).astype(jnp.bfloat16)
    rank_in = jnp.dot(present.astype(jnp.bfloat16), before_row, preferred_element_type=jnp.float32)
    rank_in = jnp.where(present > 0.5, rank_in, -1.0)
    number = jnp.sum(present, axis=1, keepdims=True)
    twos = jnp.floor((number + 1.0) * 0.5)
    square_row = lax.broadcasted_iota(jnp.int32, (blocks, blocks), 0)
    square_col = lax.broadcasted_iota(jnp.int32, (blocks, blocks), 1)
    number_row = jnp.sum(jnp.where(square_row == square_col, number, 0.0), axis=0, keepdims=True)
    twos_row = jnp.sum(jnp.where(square_row == square_col, twos, 0.0), axis=0, keepdims=True)
    start_row = jnp.sum(jnp.where(square_row < square_col, twos, 0.0), axis=0, keepdims=True)
    spot_row = lax.broadcasted_iota(jnp.int32, (TILE, TILE), 0)
    spot_col = lanes_of(TILE)
    for part in range(3):
        spot = (lax.broadcasted_iota(jnp.int32, (TILE, blocks), 0) + part * TILE).astype(jnp.float32)
        offset = spot - 2.0 * start_row
        inside = jnp.logical_and(offset >= 0.0, offset < number_row)
        member = jnp.where(inside, 1.0, 0.0).astype(jnp.bfloat16)
        wanted = jnp.sum(jnp.where(inside, offset, 0.0), axis=1, keepdims=True)
        filled = jnp.sum(jnp.where(inside, 1.0, 0.0), axis=1, keepdims=True)
        ranks = jnp.dot(member, rank_in.astype(jnp.bfloat16), preferred_element_type=jnp.float32)
        names = jnp.dot(member, which.astype(jnp.bfloat16), preferred_element_type=jnp.float32)
        chosen = jnp.sum(jnp.where(ranks == wanted, names, 0.0), axis=1, keepdims=True)
        chosen = jnp.where(filled > 0.5, jnp.minimum(chosen, 1.0 * count), 1.0 * count)
        for place_in, column in ((part, chosen), (3 + part, wanted)):
            table_buf[place_in : place_in + 1, :] = jnp.sum(
                jnp.where(spot_row == spot_col, column, 0.0), axis=0, keepdims=True
            ).astype(jnp.int32)
    empty = 1.0 * (running.shape[0] - 1)
    last_row = jnp.where(
        number_row > 0.5, jnp.minimum(start_row + twos_row - 1.0, empty), empty
    )
    table_buf[6:7, 0:blocks] = last_row.astype(jnp.int32)
    table_copy = pltpu.make_async_copy(table_buf, table, table_sem)
    table_copy.start()

    for q in range(CHUNKS):
        for i in range(1, n_feat):
            eta_copy(q, i).wait_recv()
    eta = eta_parts[lax.rem(mf, n_feat)]
    for f in range(1, n_feat):
        eta = eta + eta_parts[lax.rem(mf + n_feat - f, n_feat)]
    risk = jnp.exp(eta)
    sum_one[0] = jnp.sum(
        jnp.where(diagonal, jnp.sum(risk, axis=1, keepdims=True), 0.0), axis=0, keepdims=True
    )
    one_how = (lambda i: sum_one.at[0], sum_one, one_send, one_recv, 1)
    tm_send(*one_how)

    tm_wait(*perm_how)
    every = perm_all[:, 0, :].astype(jnp.float32)
    shard = jnp.floor(every * (1.0 / rows))
    within = every - shard * rows
    mine = jnp.logical_and(shard == me.astype(jnp.float32), lanes_of(n_tm) < rows)
    low = jnp.min(jnp.where(mine, within, 4096.0), axis=1, keepdims=True)
    high = jnp.max(jnp.where(mine, within, -1.0), axis=1, keepdims=True)
    group_low = jnp.dot(
        jnp.where(place == low, 1.0, 0.0).astype(jnp.bfloat16), group_bf,
        preferred_element_type=jnp.float32,
    )
    group_high = jnp.dot(
        jnp.where(place == high, 1.0, 0.0).astype(jnp.bfloat16), group_bf,
        preferred_element_type=jnp.float32,
    )
    for c in range(n_tm):
        group_send[c, :, 0:TILE] = group_low[c : c + 1, :]
        group_send[c, :, TILE : 2 * TILE] = group_high[c : c + 1, :]
    group_recv[0] = group_send[0]
    group_how = (lambda i: group_send.at[i], group_recv, grp_send, grp_recv, -1)
    tm_send(*group_how)

    source = lax.broadcasted_iota(jnp.int32, (TILE, TILE), 0)
    target = lanes_of(TILE)
    suffix = times_ones(risk, source >= target)
    tm_wait(*one_how)

    def add_later(c, total):
        return total + jnp.where(perm_all[c].astype(jnp.float32) > perm_col, sum_one[c], 0.0)

    after = lax.fori_loop(0, n_tm, add_later, jnp.zeros((rows, TILE), jnp.float32))
    after = jnp.sum(after, axis=1, keepdims=True)
    tm_wait(*group_how)
    shard_lane = lax.broadcasted_iota(jnp.int32, (rows, n_tm), 1).astype(jnp.float32)
    apart = my_shard - me.astype(jnp.float32)
    hit = jnp.where(shard_lane == apart + jnp.where(apart < 0.0, 1.0 * n_tm, 0.0), 1.0, 0.0)
    cohort_groups = jnp.dot(
        (hit * (1.0 - rank)).astype(jnp.bfloat16),
        group_recv[:, 0, 0:TILE].astype(jnp.bfloat16),
        preferred_element_type=jnp.float32,
    ) + jnp.dot(
        (hit * rank).astype(jnp.bfloat16),
        group_recv[:, 0, TILE : 2 * TILE].astype(jnp.bfloat16),
        preferred_element_type=jnp.float32,
    )
    later = suffix
    for k, d in enumerate(SHIFTS):
        back = pltpu.roll(cohort_groups, d, 1)
        tied = jnp.logical_and(lane >= d, back == cohort_groups)
        later = jnp.where(tied, pltpu.roll(later, d, 1), later)
    risk_total = later + after
    hazard_one = event_flag / risk_total
    hazard_two = hazard_one / risk_total
    sum_two[0] = jnp.sum(
        jnp.where(diagonal, jnp.sum(hazard_one, axis=1, keepdims=True), 0.0)
        + jnp.where(lane == row + HALF, jnp.sum(hazard_two, axis=1, keepdims=True), 0.0),
        axis=0, keepdims=True,
    )
    two_how = (lambda i: sum_two.at[0], sum_two, two_send, two_recv, 1)
    tm_send(*two_how)
    early_one = times_ones(hazard_one, source <= target)
    early_two = times_ones(hazard_two, source <= target)
    for k, d in enumerate(SHIFTS):
        ahead = pltpu.roll(cohort_groups, TILE - d, 1)
        tied = jnp.logical_and(lane < TILE - d, ahead == cohort_groups)
        early_one = jnp.where(tied, pltpu.roll(early_one, TILE - d, 1), early_one)
        early_two = jnp.where(tied, pltpu.roll(early_two, TILE - d, 1), early_two)
    tm_wait(*two_how)

    def add_early(c, total):
        return total + jnp.where(perm_all[c].astype(jnp.float32) < perm_col, sum_two[c], 0.0)

    before = lax.fori_loop(0, n_tm, add_early, jnp.zeros((rows, TILE), jnp.float32))
    cum_one = early_one + jnp.sum(
        jnp.where(lane < HALF, before, 0.0), axis=1, keepdims=True
    )
    cum_two = early_two + jnp.sum(
        jnp.where(lane < HALF, 0.0, before), axis=1, keepdims=True
    )
    resid = event_flag - risk * cum_one
    weight = risk * cum_one - risk * risk * cum_two
    for n in range(rows):
        resid_rows[n] = resid[n : n + 1, :]
        weight_rows[n] = weight[n : n + 1, :]

    table_copy.wait()
    steps = running.shape[0] - 1

    def gram_some(it, total):
        for u in range(UNROLL):
            m = it * UNROLL + u
            left, right = [], []
            for e in range(2):
                spot = 2 * m + e
                tile_at = table[lax.div(spot, TILE), lax.rem(spot, TILE)]
                tile_at = jnp.minimum(jnp.maximum(tile_at, 0), count)
                n = lax.div(tile_at, slots)
                tile = held[tile_at]
                turned = (tile.T.astype(jnp.float32) * weight_rows[n]).astype(jnp.bfloat16)
                rounded = jnp.broadcast_to(resid_rows[n], (16, TILE)).astype(jnp.bfloat16)
                left.append(jnp.concatenate([turned, rounded], axis=0))
                right.append(tile)
            keep = jnp.where(table[3 + lax.div(2 * m, TILE), lax.rem(2 * m, TILE)] > 0, 1.0, 0.0)
            total = total * keep + jnp.dot(
                jnp.concatenate(left, axis=1), jnp.concatenate(right, axis=0),
                preferred_element_type=jnp.float32,
            )
            running[m] = total
        return total

    lax.fori_loop(0, steps // UNROLL, gram_some, jnp.zeros((TILE + 16, TILE), jnp.float32))

    for q in range(CHUNKS):
        for i in range(1, n_feat):
            eta_copy(q, i).wait_send()

    lane8 = lanes_of(8)
    sub8 = lax.broadcasted_iota(jnp.int32, (8, TILE), 0)

    def pack(block, to):
        at = jnp.minimum(jnp.maximum(table[6, block], 0), steps)
        whole = running[at, 0:TILE, :]
        whole = 0.5 * (whole + whole.T)
        for i in range(7):
            width = 120 - 8 * i
            low = whole[8 * (14 - i) : 8 * (14 - i) + 8, :]
            high = pltpu.roll(whole[8 * i : 8 * i + 8, :], width, 1)
            to[8 * i : 8 * i + 8, :] = jnp.where(lane8 < width, low, high)
        grad = running[at, TILE : TILE + 8, :]
        tail = jnp.where(sub8 == 0, grad, pltpu.roll(grad, HALF, 1))
        to[56:64, :] = jnp.where(lane8 < HALF, whole[56:64, :], tail)
        to[64:72, :] = whole[120:128, :]

    half_z = n_z // 2

    def far(k):
        return half_z + jnp.where(lax.rem(k, 2) == 1, -lax.div(k + 1, 2), lax.div(k, 2))

    def pack_some(k, c):
        to_z = lax.rem(z + far(k), n_z)
        for dy in range(n_y):
            pack(to_z * n_y + lax.rem(y + dy, n_y), packed.at[k, dy])
        return c

    lax.fori_loop(0, n_z, pack_some, 0)

    half_rows = (pl.ds(0, CUT), pl.ds(CUT, PACK - CUT))
    ways = (1, n_y - 1)

    def chain_copy(k, w):
        return pltpu.make_async_remote_copy(
            src_ref=packed.at[k, 2, half_rows[w]], dst_ref=chain.at[k, half_rows[w]],
            send_sem=chain_send.at[w, k], recv_sem=chain_recv.at[w, k],
            device_id=(z * n_y + lax.rem(y + ways[w], n_y), mf), device_id_type=MESH,
        )

    def ring_copy(k, w):
        return pltpu.make_async_remote_copy(
            src_ref=packed.at[k, ways[w]], dst_ref=ring.at[w, k],
            send_sem=ring_send.at[w, k], recv_sem=ring_recv.at[w, k],
            device_id=(z * n_y + lax.rem(y + ways[w], n_y), mf), device_id_type=MESH,
        )

    def second_copy(k):
        return pltpu.make_async_remote_copy(
            src_ref=middle.at[k], dst_ref=second.at[k],
            send_sem=second_send.at[k], recv_sem=second_recv.at[k],
            device_id=(lax.rem(z + far(k), n_z) * n_y + y, mf), device_id_type=MESH,
        )

    def send_chain(k, c):
        for w in range(2):
            chain_copy(k, w).start()
        return c

    def send_ring(k, c):
        for w in range(2):
            chain_copy(k, w).wait_recv()
            packed[k, ways[w], half_rows[w], :] += chain[k, half_rows[w], :]
            ring_copy(k, w).start()
        return c

    def gathered(k):
        for w in range(2):
            ring_copy(k, w).wait_recv()
        return packed[k, 0] + ring[0, k] + ring[1, k]

    def send_second(k, c):
        middle[k] = gathered(k)
        second_copy(k).start()
        return c

    lax.fori_loop(0, n_z, send_chain, 0)
    lax.fori_loop(0, n_z, send_ring, 0)
    lax.fori_loop(0, n_z - 1, send_second, 0)
    total = gathered(n_z - 1)
    for k in range(n_z - 1):
        second_copy(k).wait_recv()
        total = total + second[k]

    pieces = [total[8 * i : 8 * i + 8, :] for i in range(9)]
    turned = pltpu.roll(pieces[7], HALF, 1)
    gradient = jnp.where(lane8[0:1] < HALF, turned[1:2, :], pieces[7][0:1, :])
    grad_row[...] = gradient
    grad_out[me] = gradient

    def gather_copy(i, src, dst, send_sem, recv_sem, incoming):
        peer = lax.rem(me + i, n_tm)
        at = peer if incoming else me
        return pltpu.make_async_remote_copy(
            src_ref=src, dst_ref=dst.at[at], send_sem=send_sem.at[peer], recv_sem=recv_sem.at[at],
            device_id=(peer, mf), device_id_type=MESH,
        )

    def send_grad(i, c):
        gather_copy(i, grad_row, grad_out, grad_send, grad_recv, False).start()
        return c

    lax.fori_loop(1, n_tm, send_grad, 0)

    tile_rows = [pltpu.roll(pieces[i], 8 + 8 * i, 1) for i in range(7)]
    tile_rows += [pieces[7]] + [pieces[14 - i] for i in range(8, 15)] + [pieces[8]]
    stacked = jnp.concatenate(tile_rows, axis=0)
    row = spot_row
    lane = spot_col
    lower = jnp.where(lane <= row, stacked, 0.0)
    upper = jnp.where(lane < row, stacked, 0.0).T
    system = lower + upper + jnp.where(lane == row, 1.0, 0.0)
    column = jnp.sum(jnp.where(lane == row, gradient, 0.0), axis=1, keepdims=True)
    solved = eliminate(system, jnp.broadcast_to(column, (TILE, TILE)))
    answer = jnp.sum(jnp.where(lane == row, solved, 0.0), axis=0, keepdims=True)
    step_row[...] = answer
    step_out[me] = answer

    def send_step(i, c):
        gather_copy(i, step_row, step_out, step_send, step_recv, False).start()
        return c

    lax.fori_loop(1, n_tm, send_step, 0)
    for k in range(n_z):
        for w in range(2):
            chain_copy(k, w).wait_send()
            ring_copy(k, w).wait_send()
        if k < n_z - 1:
            second_copy(k).wait_send()

    def finish(i, c):
        for copy in (
            gather_copy(i, grad_row, grad_out, grad_send, grad_recv, True),
            gather_copy(i, step_row, step_out, step_send, step_recv, True),
        ):
            copy.wait_recv()
            copy.wait_send()
        return c

    lax.fori_loop(1, n_tm, finish, 0)


def local(tile_data, tile_ids, owner_perm, events, groups, coefficients):
    rows, slots = tile_data.shape[:2]
    n_tm, n_feat = lax.axis_size("tm"), lax.axis_size("feat")
    n_y = Y_SIZE
    n_z = n_tm // n_y
    blocks = coefficients.shape[0] // TILE
    f32, vmem = jnp.float32, pl.BlockSpec(memory_space=pltpu.VMEM)
    smem, anywhere = pl.BlockSpec(memory_space=pltpu.SMEM), pl.BlockSpec(memory_space=pl.ANY)
    dma = pltpu.SemaphoreType.DMA
    ids = tile_ids.T
    count = rows * slots
    steps = -(-(count + blocks) // (2 * UNROLL)) * UNROLL

    gradient, step = pl.pallas_call(
        functools.partial(newton_kernel, n_z, n_y, n_feat),
        out_shape=[jax.ShapeDtypeStruct((n_tm, 1, TILE), f32)] * 2,
        in_specs=[anywhere, smem] + [anywhere] * 5,
        out_specs=[vmem, vmem],
        scratch_shapes=[
            pltpu.VMEM((count + 1, TILE, TILE), jnp.bfloat16),
            pltpu.VMEM((rows, TILE), jnp.int32),
            pltpu.VMEM((rows, TILE), jnp.int32),
            pltpu.VMEM((1, rows), jnp.int32),
            pltpu.VMEM((slots, rows), jnp.int32),
            pltpu.VMEM((blocks, TILE), jnp.bfloat16),
            pltpu.VMEM((blocks, 1, TILE), f32),
            pltpu.VMEM((rows // CHUNKS, 1, TILE), f32),
            pltpu.VMEM((n_feat, rows, TILE), f32),
            pltpu.VMEM((n_tm, 1, TILE), jnp.int32),
            pltpu.VMEM((n_tm, 1, 2 * TILE), f32),
            pltpu.VMEM((n_tm, 1, 2 * TILE), f32),
            pltpu.VMEM((n_tm, 1, TILE), f32),
            pltpu.VMEM((n_tm, 1, TILE), f32),
            pltpu.VMEM((8, TILE), jnp.int32),
            pltpu.SMEM((8, TILE), jnp.int32),
            pltpu.VMEM((rows + 1, 1, TILE), f32),
            pltpu.VMEM((rows + 1, 1, TILE), f32),
            pltpu.VMEM((steps + 1, TILE + 16, TILE), f32),
            pltpu.VMEM((n_z, n_y, PACK, TILE), f32),
            pltpu.VMEM((n_z, PACK, TILE), f32),
            pltpu.VMEM((2, n_z, PACK, TILE), f32),
            pltpu.VMEM((n_z, PACK, TILE), f32),
            pltpu.VMEM((n_z, PACK, TILE), f32),
            pltpu.VMEM((1, TILE), f32),
            pltpu.VMEM((1, TILE), f32),
            dma((CHUNKS,)), dma((5,)), dma,
            dma((CHUNKS, n_feat)), dma((CHUNKS, n_feat)),
            dma((n_tm,)), dma((n_tm,)), dma((n_tm,)), dma((n_tm,)),
            dma((n_tm,)), dma((n_tm,)), dma((n_tm,)), dma((n_tm,)),
            dma((2, n_z)), dma((2, n_z)), dma((2, n_z)), dma((2, n_z)), dma((n_z,)), dma((n_z,)),
            dma((n_tm,)), dma((n_tm,)), dma((n_tm,)), dma((n_tm,)),
        ],
        compiler_params=pltpu.CompilerParams(
            collective_id=0, has_side_effects=True, vmem_limit_bytes=60 * 2**20
        ),
        name="newton",
    )(
        tile_data.reshape(count, TILE, TILE), ids, ids, owner_perm.reshape(1, rows),
        events, groups, coefficients.reshape(blocks, TILE),
    )
    return gradient.reshape(-1), step.reshape(-1)


def solution(mesh):
    return jax.shard_map(
        local,
        mesh=mesh,
        in_specs=(
            P("tm", "feat", None, None),
            P("tm", "feat"),
            P("tm"),
            P("tm", None),
            P("tm", None),
            P("feat"),
        ),
        out_specs=(P("feat"), P("feat")),
        check_vma=False,
    )
```

```python
import functools

import jax
import jax.numpy as jnp
from jax import lax
from jax.experimental import pallas as pl
from jax.experimental.pallas import tpu as pltpu
from jax.sharding import PartitionSpec as P

MESH = pl.DeviceIdType.MESH
TILE = 128
HALF = 64
PACK = 72
SHIFTS = (1, 2, 4, 8, 16, 32, 64)
Y_SIZE = 4
CHUNKS = 4
CUT = 40
UNROLL = 18


def lanes_of(rows):
    return lax.broadcasted_iota(jnp.int32, (rows, TILE), 1)


def three_parts(x):
    high = x.astype(jnp.bfloat16)
    rest = x - high.astype(jnp.float32)
    mid = rest.astype(jnp.bfloat16)
    low = (rest - mid.astype(jnp.float32)).astype(jnp.bfloat16)
    return high, mid, low


def times_ones(x, mask):
    rows = x.shape[0]
    out = jnp.dot(
        jnp.concatenate(three_parts(x), axis=0),
        jnp.where(mask, 1.0, 0.0).astype(jnp.bfloat16),
        preferred_element_type=jnp.float32,
    )
    return out[2 * rows :] + out[rows : 2 * rows] + out[:rows]


def eliminate(system, rhs, wide=32):
    tiles = wide // 8
    sub = lax.broadcasted_iota(jnp.int32, (8, TILE), 0)

    def spread(x, r):
        return jnp.broadcast_to(x[r : r + 1, :], (8, TILE))

    def panel(p, carry):
        whole, right = carry
        a = [whole[8 * i : 8 * i + 8, :] for i in range(tiles)]
        g = [right[8 * i : 8 * i + 8, :] for i in range(tiles)]
        for q in range(tiles):
            cols = [
                [
                    jnp.broadcast_to(a[i][:, 8 * q + r : 8 * q + r + 1], (8, TILE))
                    for i in range(tiles)
                ]
                for r in range(8)
            ]
            head = [cols[r][q] for r in range(8)]
            top, top_g = a[q], g[q]
            for r in range(8):
                inverse = 1.0 / spread(head[r], r)
                factor = jnp.where(sub == r, 1.0 - inverse, head[r] * inverse)
                for k in range(r + 1, 8):
                    head[k] = head[k] - factor * spread(head[k], r)
                top = top - factor * spread(top, r)
                top_g = top_g - factor * spread(top_g, r)
            for i in range(tiles):
                if i != q:
                    for r in range(8):
                        a[i] = a[i] - cols[r][i] * spread(top, r)
                        g[i] = g[i] - cols[r][i] * spread(top_g, r)
            a[q], g[q] = top, top_g
        done, done_g = jnp.concatenate(a, axis=0), jnp.concatenate(g, axis=0)
        rest = whole[wide:, :]
        update = jnp.dot(
            rest[:, :wide], jnp.concatenate([done, done_g], axis=1),
            precision=lax.Precision.HIGHEST, preferred_element_type=jnp.float32,
        )
        whole = jnp.concatenate([rest - update[:, :TILE], done], axis=0)
        right = jnp.concatenate([right[wide:, :] - update[:, TILE:], done_g], axis=0)
        return pltpu.roll(whole, TILE - wide, 1), right

    return lax.fori_loop(0, TILE // wide, panel, (system, rhs))[1]


def newton_kernel(
    n_z, n_y, n_feat,
    tiles, ids, id_rows, perm, events, groups, coef,
    grad_out, step_out,
    held, event_buf, group_buf, perm_buf, id_buf, coef_buf, coef_wide, eta_rows,
    eta_parts, perm_all, group_send, group_recv, sum_one, sum_two,
    table_buf, table, weight_rows, resid_rows, running,
    packed, chain, ring, middle, second, grad_row, step_row,
    tile_sem, small_sem, table_sem, eta_send, eta_recv, perm_send, perm_recv, grp_send, grp_recv,
    one_send, one_recv, two_send, two_recv,
    chain_send, chain_recv, ring_send, ring_recv, second_send, second_recv,
    grad_send, grad_recv, step_send, step_recv,
):
    n_tm = n_z * n_y
    z = lax.div(lax.axis_index("tm"), n_y)
    y = lax.rem(lax.axis_index("tm"), n_y)
    me = lax.axis_index("tm")
    mf = lax.axis_index("feat")
    rows = events.shape[0]
    per = rows // CHUNKS
    slots, blocks = id_rows.shape[0], coef.shape[0]
    count = rows * slots
    barrier = pltpu.get_barrier_semaphore()

    def outward(k, size):
        return size // 2 + jnp.where(lax.rem(k, 2) == 1, -lax.div(k + 1, 2), lax.div(k, 2))

    def greet_tm(k, c):
        peer = lax.rem(me + outward(k, n_tm), n_tm)
        pl.semaphore_signal(barrier, inc=1, device_id=(peer, mf), device_id_type=MESH)
        return c

    def greet_feat(k, c):
        peer = lax.rem(mf + outward(k, n_feat), n_feat)
        pl.semaphore_signal(barrier, inc=1, device_id=(me, peer), device_id_type=MESH)
        return c

    def tile_copy(q):
        part = pl.ds(q * per * slots, per * slots)
        return pltpu.make_async_copy(tiles.at[part], held.at[part], tile_sem.at[q])

    small = [
        pltpu.make_async_copy(source, target, small_sem.at[k])
        for k, (source, target) in enumerate(
            ((coef, coef_buf), (perm, perm_buf), (groups, group_buf), (events, event_buf), (id_rows, id_buf))
        )
    ]
    lax.fori_loop(0, n_tm - 1, greet_tm, 0)
    lax.fori_loop(0, n_feat - 1, greet_feat, 0)
    small[0].start()
    for q in range(CHUNKS):
        tile_copy(q).start()
    for copy in small[1:]:
        copy.start()

    def tm_send(source, target, send_sem, recv_sem, sign):
        def one(k, c):
            i = outward(k, n_tm)
            pltpu.make_async_remote_copy(
                src_ref=source(i), dst_ref=target.at[i], send_sem=send_sem, recv_sem=recv_sem,
                device_id=(lax.rem(me + sign * i + n_tm, n_tm), mf), device_id_type=MESH,
            ).start()
            return c

        lax.fori_loop(0, n_tm - 1, one, 0)

    def all_of(target, send_sem, recv_sem, size):
        places = target.at[pl.ds(1, size - 1)]
        return pltpu.make_async_remote_copy(
            src_ref=places, dst_ref=places, send_sem=send_sem, recv_sem=recv_sem,
            device_id=(lax.rem(me + 1, n_tm), mf), device_id_type=MESH,
        )

    def tm_wait(source, target, send_sem, recv_sem, sign):
        copy = all_of(target, send_sem, recv_sem, n_tm)
        copy.wait_recv()
        copy.wait_send()

    small[0].wait()
    wide = coef_buf[...].astype(jnp.float32)
    for j in range(blocks):
        coef_wide[j] = wide[j : j + 1, :]

    def eta_make(q):
        tile_copy(q).wait()
        together = min(4, per)

        def some(k, c):
            for u in range(together):
                i = k * together + u
                n = q * per + i
                total = None
                for s in range(slots):
                    term = held[n * slots + s].astype(jnp.float32) * coef_wide[ids[s, n]]
                    total = term if total is None else total + term
                eta_rows[i] = jnp.sum(total.T, axis=0, keepdims=True)
            return c

        lax.fori_loop(0, per // together, some, 0)
        eta_parts[0, q * per : (q + 1) * per, :] = jnp.concatenate(
            [eta_rows[i] for i in range(per)], axis=0
        )

    def eta_start(k, c):
        i = outward(k, n_feat)
        pltpu.make_async_remote_copy(
            src_ref=eta_parts.at[0], dst_ref=eta_parts.at[i], send_sem=eta_send, recv_sem=eta_recv,
            device_id=(me, lax.rem(mf + i, n_feat)), device_id_type=MESH,
        ).start()
        return c

    lane = lanes_of(rows)
    row = lax.broadcasted_iota(jnp.int32, (rows, TILE), 0)
    diagonal = lane == row
    for q in range(CHUNKS):
        eta_make(q)
    for copy in small[1:]:
        copy.wait()
    gap = jnp.zeros((1, HALF - rows), jnp.int32)
    perm_all[0] = jnp.concatenate(
        [perm_buf[...], gap] * 2 if rows < HALF else [perm_buf[...]] * 2, axis=1
    )

    held[count] = jnp.zeros((TILE, TILE), jnp.bfloat16)
    resid_rows[rows] = jnp.zeros((1, TILE), jnp.float32)
    weight_rows[rows] = jnp.zeros((1, TILE), jnp.float32)
    running[running.shape[0] - 1] = jnp.zeros(running.shape[1:], jnp.float32)
    table_buf[...] = jnp.zeros_like(table_buf)

    event_flag = event_buf[...].astype(jnp.float32)
    group_bf = group_buf[...].astype(jnp.float32).astype(jnp.bfloat16)
    place = lax.broadcasted_iota(jnp.int32, (n_tm, rows), 1).astype(jnp.float32)
    perm_row = perm_all[0].astype(jnp.float32)
    perm_col = jnp.sum(jnp.where(diagonal, perm_row, 0.0), axis=1, keepdims=True)
    my_shard = jnp.floor(perm_col * (1.0 / rows))
    same = jnp.logical_and(jnp.floor(perm_row * (1.0 / rows)) == my_shard, perm_row < perm_col)
    rank = jnp.sum(
        jnp.where(jnp.logical_and(same, lane < rows), 1.0, 0.0), axis=1, keepdims=True
    )
    id_all = id_buf[...]
    block_at = lax.broadcasted_iota(jnp.int32, (blocks, rows), 0)
    row_at = lax.broadcasted_iota(jnp.int32, (blocks, rows), 1)
    present = jnp.zeros((blocks, rows), jnp.float32)
    which = jnp.zeros((blocks, rows), jnp.float32)
    for s in range(slots):
        here = id_all[s : s + 1, :] == block_at
        present = present + jnp.where(here, 1.0, 0.0)
        which = which + jnp.where(here, (row_at * slots + s).astype(jnp.float32), 0.0)
    before_row = jnp.where(
        lax.broadcasted_iota(jnp.int32, (rows, rows), 0)
        < lax.broadcasted_iota(jnp.int32, (rows, rows), 1), 1.0, 0.0,
    ).astype(jnp.bfloat16)
    rank_in = jnp.dot(present.astype(jnp.bfloat16), before_row, preferred_element_type=jnp.float32)
    rank_in = jnp.where(present > 0.5, rank_in, -1.0)
    number = jnp.sum(present, axis=1, keepdims=True)
    twos = jnp.floor((number + 1.0) * 0.5)
    square_row = lax.broadcasted_iota(jnp.int32, (blocks, blocks), 0)
    square_col = lax.broadcasted_iota(jnp.int32, (blocks, blocks), 1)
    number_row = jnp.sum(jnp.where(square_row == square_col, number, 0.0), axis=0, keepdims=True)
    twos_row = jnp.sum(jnp.where(square_row == square_col, twos, 0.0), axis=0, keepdims=True)
    start_row = jnp.sum(jnp.where(square_row < square_col, twos, 0.0), axis=0, keepdims=True)
    spot_row = lax.broadcasted_iota(jnp.int32, (TILE, TILE), 0)
    spot_col = lanes_of(TILE)
    for part in range(3):
        spot = (lax.broadcasted_iota(jnp.int32, (TILE, blocks), 0) + part * TILE).astype(jnp.float32)
        offset = spot - 2.0 * start_row
        inside = jnp.logical_and(offset >= 0.0, offset < number_row)
        member = jnp.where(inside, 1.0, 0.0).astype(jnp.bfloat16)
        wanted = jnp.sum(jnp.where(inside, offset, 0.0), axis=1, keepdims=True)
        filled = jnp.sum(jnp.where(inside, 1.0, 0.0), axis=1, keepdims=True)
        ranks = jnp.dot(member, rank_in.astype(jnp.bfloat16), preferred_element_type=jnp.float32)
        names = jnp.dot(member, which.astype(jnp.bfloat16), preferred_element_type=jnp.float32)
        chosen = jnp.sum(jnp.where(ranks == wanted, names, 0.0), axis=1, keepdims=True)
        chosen = jnp.where(filled > 0.5, jnp.minimum(chosen, 1.0 * count), 1.0 * count)
        for place_in, column in ((part, chosen), (3 + part, wanted)):
            table_buf[place_in : place_in + 1, :] = jnp.sum(
                jnp.where(spot_row == spot_col, column, 0.0), axis=0, keepdims=True
            ).astype(jnp.int32)
    empty = 1.0 * (running.shape[0] - 1)
    last_row = jnp.where(
        number_row > 0.5, jnp.minimum(start_row + twos_row - 1.0, empty), empty
    )
    table_buf[6:7, 0:blocks] = last_row.astype(jnp.int32)
    table_copy = pltpu.make_async_copy(table_buf, table, table_sem)
    table_copy.start()

    pl.semaphore_wait(barrier, n_tm + n_feat - 2)
    lax.fori_loop(0, n_feat - 1, eta_start, 0)
    perm_how = (lambda i: perm_all.at[0], perm_all, perm_send, perm_recv, 1)
    tm_send(*perm_how)

    if n_feat > 1:
        eta_all = all_of(eta_parts, eta_send, eta_recv, n_feat)
        eta_all.wait_recv()
        eta_all.wait_send()
    eta = eta_parts[lax.rem(mf, n_feat)]
    for f in range(1, n_feat):
        eta = eta + eta_parts[lax.rem(mf + n_feat - f, n_feat)]
    risk = jnp.exp(eta)
    sum_one[0] = jnp.sum(
        jnp.where(diagonal, jnp.sum(risk, axis=1, keepdims=True), 0.0), axis=0, keepdims=True
    )
    one_how = (lambda i: sum_one.at[0], sum_one, one_send, one_recv, 1)
    tm_send(*one_how)

    tm_wait(*perm_how)
    every = perm_all[:, 0, :].astype(jnp.float32)
    shard = jnp.floor(every * (1.0 / rows))
    within = every - shard * rows
    mine = jnp.logical_and(shard == me.astype(jnp.float32), lanes_of(n_tm) < rows)
    low = jnp.min(jnp.where(mine, within, 4096.0), axis=1, keepdims=True)
    high = jnp.max(jnp.where(mine, within, -1.0), axis=1, keepdims=True)
    group_low = jnp.dot(
        jnp.where(place == low, 1.0, 0.0).astype(jnp.bfloat16), group_bf,
        preferred_element_type=jnp.float32,
    )
    group_high = jnp.dot(
        jnp.where(place == high, 1.0, 0.0).astype(jnp.bfloat16), group_bf,
        preferred_element_type=jnp.float32,
    )
    for c in range(n_tm):
        group_send[c, :, 0:TILE] = group_low[c : c + 1, :]
        group_send[c, :, TILE : 2 * TILE] = group_high[c : c + 1, :]
    group_recv[0] = group_send[0]
    group_how = (lambda i: group_send.at[i], group_recv, grp_send, grp_recv, -1)
    tm_send(*group_how)

    source = lax.broadcasted_iota(jnp.int32, (TILE, TILE), 0)
    target = lanes_of(TILE)
    suffix = times_ones(risk, source >= target)
    tm_wait(*one_how)

    def add_later(c, total):
        return total + jnp.where(perm_all[c].astype(jnp.float32) > perm_col, sum_one[c], 0.0)

    after = lax.fori_loop(0, n_tm, add_later, jnp.zeros((rows, TILE), jnp.float32))
    after = jnp.sum(after, axis=1, keepdims=True)
    tm_wait(*group_how)
    shard_lane = lax.broadcasted_iota(jnp.int32, (rows, n_tm), 1).astype(jnp.float32)
    apart = my_shard - me.astype(jnp.float32)
    hit = jnp.where(shard_lane == apart + jnp.where(apart < 0.0, 1.0 * n_tm, 0.0), 1.0, 0.0)
    cohort_groups = jnp.dot(
        (hit * (1.0 - rank)).astype(jnp.bfloat16),
        group_recv[:, 0, 0:TILE].astype(jnp.bfloat16),
        preferred_element_type=jnp.float32,
    ) + jnp.dot(
        (hit * rank).astype(jnp.bfloat16),
        group_recv[:, 0, TILE : 2 * TILE].astype(jnp.bfloat16),
        preferred_element_type=jnp.float32,
    )
    later = suffix
    for k, d in enumerate(SHIFTS):
        back = pltpu.roll(cohort_groups, d, 1)
        tied = jnp.logical_and(lane >= d, back == cohort_groups)
        later = jnp.where(tied, pltpu.roll(later, d, 1), later)
    risk_total = later + after
    hazard_one = event_flag / risk_total
    hazard_two = hazard_one / risk_total
    sum_two[0] = jnp.sum(
        jnp.where(diagonal, jnp.sum(hazard_one, axis=1, keepdims=True), 0.0)
        + jnp.where(lane == row + HALF, jnp.sum(hazard_two, axis=1, keepdims=True), 0.0),
        axis=0, keepdims=True,
    )
    two_how = (lambda i: sum_two.at[0], sum_two, two_send, two_recv, 1)
    tm_send(*two_how)
    early_one = times_ones(hazard_one, source <= target)
    early_two = times_ones(hazard_two, source <= target)
    for k, d in enumerate(SHIFTS):
        ahead = pltpu.roll(cohort_groups, TILE - d, 1)
        tied = jnp.logical_and(lane < TILE - d, ahead == cohort_groups)
        early_one = jnp.where(tied, pltpu.roll(early_one, TILE - d, 1), early_one)
        early_two = jnp.where(tied, pltpu.roll(early_two, TILE - d, 1), early_two)
    tm_wait(*two_how)

    def add_early(c, total):
        return total + jnp.where(perm_all[c].astype(jnp.float32) < perm_col, sum_two[c], 0.0)

    before = lax.fori_loop(0, n_tm, add_early, jnp.zeros((rows, TILE), jnp.float32))
    cum_one = early_one + jnp.sum(
        jnp.where(lane < HALF, before, 0.0), axis=1, keepdims=True
    )
    cum_two = early_two + jnp.sum(
        jnp.where(lane < HALF, 0.0, before), axis=1, keepdims=True
    )
    resid = event_flag - risk * cum_one
    weight = risk * cum_one - risk * risk * cum_two
    for n in range(rows):
        resid_rows[n] = resid[n : n + 1, :]
        weight_rows[n] = weight[n : n + 1, :]

    table_copy.wait()
    steps = running.shape[0] - 1

    def gram_some(it, total):
        for u in range(UNROLL):
            m = it * UNROLL + u
            left, right = [], []
            for e in range(2):
                spot = 2 * m + e
                tile_at = table[lax.div(spot, TILE), lax.rem(spot, TILE)]
                tile_at = jnp.minimum(jnp.maximum(tile_at, 0), count)
                n = lax.div(tile_at, slots)
                tile = held[tile_at]
                turned = (tile.T.astype(jnp.float32) * weight_rows[n]).astype(jnp.bfloat16)
                rounded = jnp.broadcast_to(resid_rows[n], (16, TILE)).astype(jnp.bfloat16)
                left.append(jnp.concatenate([turned, rounded], axis=0))
                right.append(tile)
            keep = jnp.where(table[3 + lax.div(2 * m, TILE), lax.rem(2 * m, TILE)] > 0, 1.0, 0.0)
            total = total * keep + jnp.dot(
                jnp.concatenate(left, axis=1), jnp.concatenate(right, axis=0),
                preferred_element_type=jnp.float32,
            )
            running[m] = total
        return total

    lax.fori_loop(0, steps // UNROLL, gram_some, jnp.zeros((TILE + 16, TILE), jnp.float32))

    lane8 = lanes_of(8)
    sub8 = lax.broadcasted_iota(jnp.int32, (8, TILE), 0)

    def pack(block, to):
        at = jnp.minimum(jnp.maximum(table[6, block], 0), steps)
        whole = running[at, 0:TILE, :]
        whole = 0.5 * (whole + whole.T)
        for i in range(7):
            width = 120 - 8 * i
            low = whole[8 * (14 - i) : 8 * (14 - i) + 8, :]
            high = pltpu.roll(whole[8 * i : 8 * i + 8, :], width, 1)
            to[8 * i : 8 * i + 8, :] = jnp.where(lane8 < width, low, high)
        grad = running[at, TILE : TILE + 8, :]
        tail = jnp.where(sub8 == 0, grad, pltpu.roll(grad, HALF, 1))
        to[56:64, :] = jnp.where(lane8 < HALF, whole[56:64, :], tail)
        to[64:72, :] = whole[120:128, :]

    half_z = n_z // 2

    def far(k):
        return half_z + jnp.where(lax.rem(k, 2) == 1, -lax.div(k + 1, 2), lax.div(k, 2))

    def pack_for(k, dy):
        pack(lax.rem(z + far(k), n_z) * n_y + lax.rem(y + dy, n_y), packed.at[k, dy])

    half_rows = (pl.ds(0, CUT), pl.ds(CUT, PACK - CUT))
    ways = (1, n_y - 1)

    def chain_copy(k, w):
        return pltpu.make_async_remote_copy(
            src_ref=packed.at[k, 2, half_rows[w]], dst_ref=chain.at[k, half_rows[w]],
            send_sem=chain_send.at[w], recv_sem=chain_recv.at[w, k],
            device_id=(z * n_y + lax.rem(y + ways[w], n_y), mf), device_id_type=MESH,
        )

    def ring_copy(k, w):
        return pltpu.make_async_remote_copy(
            src_ref=packed.at[k, ways[w]], dst_ref=ring.at[w, k],
            send_sem=ring_send.at[w], recv_sem=ring_recv.at[w, k],
            device_id=(z * n_y + lax.rem(y + ways[w], n_y), mf), device_id_type=MESH,
        )

    def second_copy(k):
        return pltpu.make_async_remote_copy(
            src_ref=middle.at[k], dst_ref=second.at[k],
            send_sem=second_send, recv_sem=second_recv,
            device_id=(lax.rem(z + far(k), n_z) * n_y + y, mf), device_id_type=MESH,
        )

    def send_chain(k, c):
        pack_for(k, 2)
        for w in range(2):
            chain_copy(k, w).start()
        return c

    def send_ring(k, c):
        pack_for(k, 1)
        pack_for(k, 3)
        for w in range(2):
            chain_copy(k, w).wait_recv()
            packed[k, ways[w], half_rows[w], :] += chain[k, half_rows[w], :]
            ring_copy(k, w).start()
        return c

    def pack_own(k, c):
        pack_for(k, 0)
        return c

    def gathered(k):
        for w in range(2):
            ring_copy(k, w).wait_recv()
        return packed[k, 0] + ring[0, k] + ring[1, k]

    def send_second(k, c):
        middle[k] = gathered(k)
        second_copy(k).start()
        return c

    lax.fori_loop(0, n_z, send_chain, 0)
    lax.fori_loop(0, n_z, send_ring, 0)
    lax.fori_loop(0, n_z, pack_own, 0)
    lax.fori_loop(0, n_z - 1, send_second, 0)
    total = gathered(n_z - 1)
    second_all = all_of(second, second_send, second_recv, n_z)
    second_all.wait_recv()
    for k in range(n_z - 1):
        total = total + second[k]

    pieces = [total[8 * i : 8 * i + 8, :] for i in range(9)]
    turned = pltpu.roll(pieces[7], HALF, 1)
    gradient = jnp.where(lane8[0:1] < HALF, turned[1:2, :], pieces[7][0:1, :])
    grad_row[...] = gradient
    grad_out[me] = gradient

    def send_block(source, target, send_sem, recv_sem):
        def one(k, c):
            peer = lax.rem(me + outward(k, n_tm), n_tm)
            pltpu.make_async_remote_copy(
                src_ref=source, dst_ref=target.at[me], send_sem=send_sem, recv_sem=recv_sem,
                device_id=(peer, mf), device_id_type=MESH,
            ).start()
            return c

        lax.fori_loop(0, n_tm - 1, one, 0)

    send_block(grad_row, grad_out, grad_send, grad_recv)

    tile_rows = [pltpu.roll(pieces[i], 8 + 8 * i, 1) for i in range(7)]
    tile_rows += [pieces[7]] + [pieces[14 - i] for i in range(8, 15)] + [pieces[8]]
    stacked = jnp.concatenate(tile_rows, axis=0)
    row = spot_row
    lane = spot_col
    lower = jnp.where(lane <= row, stacked, 0.0)
    upper = jnp.where(lane < row, stacked, 0.0).T
    system = lower + upper + jnp.where(lane == row, 1.0, 0.0)
    column = jnp.sum(jnp.where(lane == row, gradient, 0.0), axis=1, keepdims=True)
    solved = eliminate(system, jnp.broadcast_to(column, (TILE, TILE)))
    answer = jnp.sum(jnp.where(lane == row, solved, 0.0), axis=0, keepdims=True)
    step_row[...] = answer
    step_out[me] = answer

    send_block(step_row, step_out, step_send, step_recv)
    for w in range(2):
        for sent, send_sem, recv_sem in (
            (chain.at[pl.ds(0, n_z), half_rows[w]], chain_send.at[w], chain_recv.at[w, 0]),
            (ring.at[w], ring_send.at[w], ring_recv.at[w, 0]),
        ):
            pltpu.make_async_remote_copy(
                src_ref=sent, dst_ref=sent, send_sem=send_sem, recv_sem=recv_sem,
                device_id=(lax.rem(me + 1, n_tm), mf), device_id_type=MESH,
            ).wait_send()
    second_all.wait_send()
    for target, send_sem, recv_sem in (
        (grad_out, grad_send, grad_recv), (step_out, step_send, step_recv),
    ):
        copy = all_of(target, send_sem, recv_sem, n_tm)
        copy.wait_recv()
        copy.wait_send()


def local(tile_data, tile_ids, owner_perm, events, groups, coefficients):
    rows, slots = tile_data.shape[:2]
    n_tm, n_feat = lax.axis_size("tm"), lax.axis_size("feat")
    n_y = Y_SIZE
    n_z = n_tm // n_y
    blocks = coefficients.shape[0] // TILE
    f32, vmem = jnp.float32, pl.BlockSpec(memory_space=pltpu.VMEM)
    smem, anywhere = pl.BlockSpec(memory_space=pltpu.SMEM), pl.BlockSpec(memory_space=pl.ANY)
    dma = pltpu.SemaphoreType.DMA
    ids = tile_ids.T
    count = rows * slots
    steps = -(-(count + blocks) // (2 * UNROLL)) * UNROLL

    gradient, step = pl.pallas_call(
        functools.partial(newton_kernel, n_z, n_y, n_feat),
        out_shape=[jax.ShapeDtypeStruct((n_tm, 1, TILE), f32)] * 2,
        in_specs=[anywhere, smem] + [anywhere] * 5,
        out_specs=[vmem, vmem],
        scratch_shapes=[
            pltpu.VMEM((count + 1, TILE, TILE), jnp.bfloat16),
            pltpu.VMEM((rows, TILE), jnp.int32),
            pltpu.VMEM((rows, TILE), jnp.int32),
            pltpu.VMEM((1, rows), jnp.int32),
            pltpu.VMEM((slots, rows), jnp.int32),
            pltpu.VMEM((blocks, TILE), jnp.bfloat16),
            pltpu.VMEM((blocks, 1, TILE), f32),
            pltpu.VMEM((rows // CHUNKS, 1, TILE), f32),
            pltpu.VMEM((n_feat, rows, TILE), f32),
            pltpu.VMEM((n_tm, 1, TILE), jnp.int32),
            pltpu.VMEM((n_tm, 1, 2 * TILE), f32),
            pltpu.VMEM((n_tm, 1, 2 * TILE), f32),
            pltpu.VMEM((n_tm, 1, TILE), f32),
            pltpu.VMEM((n_tm, 1, TILE), f32),
            pltpu.VMEM((8, TILE), jnp.int32),
            pltpu.SMEM((8, TILE), jnp.int32),
            pltpu.VMEM((rows + 1, 1, TILE), f32),
            pltpu.VMEM((rows + 1, 1, TILE), f32),
            pltpu.VMEM((steps + 1, TILE + 16, TILE), f32),
            pltpu.VMEM((n_z, n_y, PACK, TILE), f32),
            pltpu.VMEM((n_z, PACK, TILE), f32),
            pltpu.VMEM((2, n_z, PACK, TILE), f32),
            pltpu.VMEM((n_z, PACK, TILE), f32),
            pltpu.VMEM((n_z, PACK, TILE), f32),
            pltpu.VMEM((1, TILE), f32),
            pltpu.VMEM((1, TILE), f32),
            dma((CHUNKS,)), dma((5,)), dma,
            dma, dma, dma, dma, dma, dma, dma, dma, dma, dma,
            dma((2,)), dma((2, n_z)), dma((2,)), dma((2, n_z)), dma, dma,
            dma, dma, dma, dma,
        ],
        compiler_params=pltpu.CompilerParams(
            collective_id=0, has_side_effects=True, vmem_limit_bytes=60 * 2**20
        ),
        name="newton",
    )(
        tile_data.reshape(count, TILE, TILE), ids, ids, owner_perm.reshape(1, rows),
        events, groups, coefficients.reshape(blocks, TILE),
    )
    return gradient.reshape(-1), step.reshape(-1)


def solution(mesh):
    return jax.shard_map(
        local,
        mesh=mesh,
        in_specs=(
            P("tm", "feat", None, None),
            P("tm", "feat"),
            P("tm"),
            P("tm", None),
            P("tm", None),
            P("feat"),
        ),
        out_specs=(P("feat"), P("feat")),
        check_vma=False,
    )
```

```python
import functools

import jax
import jax.numpy as jnp
from jax import lax
from jax.experimental import pallas as pl
from jax.experimental.pallas import tpu as pltpu
from jax.sharding import PartitionSpec as P

MESH = pl.DeviceIdType.MESH
TILE = 128
HALF = 64
PACK = 72
SHIFTS = (1, 2, 4, 8, 16, 32, 64)
Y_SIZE = 4
CHUNKS = 4
CUT = 40
UNROLL = 18


def lanes_of(rows):
    return lax.broadcasted_iota(jnp.int32, (rows, TILE), 1)


def three_parts(x):
    high = x.astype(jnp.bfloat16)
    rest = x - high.astype(jnp.float32)
    mid = rest.astype(jnp.bfloat16)
    low = (rest - mid.astype(jnp.float32)).astype(jnp.bfloat16)
    return high, mid, low


def times_ones(x, mask):
    rows = x.shape[0]
    out = jnp.dot(
        jnp.concatenate(three_parts(x), axis=0),
        jnp.where(mask, 1.0, 0.0).astype(jnp.bfloat16),
        preferred_element_type=jnp.float32,
    )
    return out[2 * rows :] + out[rows : 2 * rows] + out[:rows]


def eliminate(system, rhs, wide=32):
    tiles = wide // 8
    sub = lax.broadcasted_iota(jnp.int32, (8, TILE), 0)

    def spread(x, r):
        return jnp.broadcast_to(x[r : r + 1, :], (8, TILE))

    def panel(p, carry):
        whole, right = carry
        a = [whole[8 * i : 8 * i + 8, :] for i in range(tiles)]
        g = [right[8 * i : 8 * i + 8, :] for i in range(tiles)]
        for q in range(tiles):
            cols = [
                [
                    jnp.broadcast_to(a[i][:, 8 * q + r : 8 * q + r + 1], (8, TILE))
                    for i in range(tiles)
                ]
                for r in range(8)
            ]
            head = [cols[r][q] for r in range(8)]
            top, top_g = a[q], g[q]
            for r in range(8):
                inverse = 1.0 / spread(head[r], r)
                factor = jnp.where(sub == r, inverse, -(head[r] * inverse))

                def step(x, r=r, factor=factor):
                    return jnp.where(sub == r, 0.0, x) + factor * spread(x, r)

                for k in range(r + 1, 8):
                    head[k] = step(head[k])
                top, top_g = step(top), step(top_g)
            for i in range(tiles):
                if i != q:
                    for r in range(8):
                        a[i] = a[i] - cols[r][i] * spread(top, r)
                        g[i] = g[i] - cols[r][i] * spread(top_g, r)
            a[q], g[q] = top, top_g
        done, done_g = jnp.concatenate(a, axis=0), jnp.concatenate(g, axis=0)
        rest = whole[wide:, :]
        update = jnp.dot(
            rest[:, :wide], jnp.concatenate([done, done_g], axis=1),
            precision=lax.Precision.HIGHEST, preferred_element_type=jnp.float32,
        )
        whole = jnp.concatenate([rest - update[:, :TILE], done], axis=0)
        right = jnp.concatenate([right[wide:, :] - update[:, TILE:], done_g], axis=0)
        return pltpu.roll(whole, TILE - wide, 1), right

    return lax.fori_loop(0, TILE // wide, panel, (system, rhs))[1]


def newton_kernel(
    n_z, n_y, n_feat,
    tiles, ids, id_rows, perm, events, groups, coef,
    grad_out, step_out,
    held, event_buf, group_buf, perm_buf, id_buf, coef_buf, coef_wide, eta_rows,
    eta_parts, eta_chips, perm_all, group_send, group_recv, sum_one, sum_two,
    table_buf, table, weight_rows, resid_rows, running,
    packed, chain, ring, middle, second, grad_row, step_row,
    tile_sem, small_sem, table_sem, pair_send, pair_recv, eta_send, eta_recv, perm_send, perm_recv, grp_send, grp_recv,
    one_send, one_recv, two_send, two_recv,
    chain_send, chain_recv, ring_send, ring_recv, second_send, second_recv,
    grad_send, grad_recv, step_send, step_recv, own_sem,
):
    n_tm = n_z * n_y
    z = lax.div(lax.axis_index("tm"), n_y)
    y = lax.rem(lax.axis_index("tm"), n_y)
    me = lax.axis_index("tm")
    mf = lax.axis_index("feat")
    rows = events.shape[0]
    per = rows // CHUNKS
    slots, blocks = id_rows.shape[0], coef.shape[0]
    count = rows * slots
    barrier = pltpu.get_barrier_semaphore()

    def outward(k, size):
        return size // 2 + jnp.where(lax.rem(k, 2) == 1, -lax.div(k + 1, 2), lax.div(k, 2))

    def greet_tm(k, c):
        peer = lax.rem(me + outward(k, n_tm), n_tm)
        pl.semaphore_signal(barrier, inc=1, device_id=(peer, mf), device_id_type=MESH)
        return c

    def greet_feat(k, c):
        peer = lax.rem(mf + outward(k, n_feat), n_feat)
        pl.semaphore_signal(barrier, inc=1, device_id=(me, peer), device_id_type=MESH)
        return c

    def tile_copy(q):
        part = pl.ds(q * per * slots, per * slots)
        return pltpu.make_async_copy(tiles.at[part], held.at[part], tile_sem.at[q])

    small = [
        pltpu.make_async_copy(source, target, small_sem.at[k])
        for k, (source, target) in enumerate(
            ((coef, coef_buf), (perm, perm_buf), (groups, group_buf), (events, event_buf), (id_rows, id_buf))
        )
    ]
    lax.fori_loop(0, n_tm - 1, greet_tm, 0)
    lax.fori_loop(0, n_feat - 1, greet_feat, 0)
    small[0].start()
    for q in range(CHUNKS):
        tile_copy(q).start()
    for copy in small[1:]:
        copy.start()

    def tm_send(source, target, send_sem, recv_sem, sign):
        def one(k, c):
            i = outward(k, n_tm)
            pltpu.make_async_remote_copy(
                src_ref=source(i), dst_ref=target.at[i], send_sem=send_sem, recv_sem=recv_sem,
                device_id=(lax.rem(me + sign * i + n_tm, n_tm), mf), device_id_type=MESH,
            ).start()
            return c

        lax.fori_loop(0, n_tm - 1, one, 0)

    def all_of(target, send_sem, recv_sem, size):
        places = target.at[pl.ds(1, size - 1)]
        return pltpu.make_async_remote_copy(
            src_ref=places, dst_ref=places, send_sem=send_sem, recv_sem=recv_sem,
            device_id=(lax.rem(me + 1, n_tm), mf), device_id_type=MESH,
        )

    def tm_wait(source, target, send_sem, recv_sem, sign):
        copy = all_of(target, send_sem, recv_sem, n_tm)
        copy.wait_recv()
        copy.wait_send()

    small[0].wait()
    wide = coef_buf[...].astype(jnp.float32)
    for j in range(blocks):
        coef_wide[j] = wide[j : j + 1, :]

    def eta_make(q):
        tile_copy(q).wait()
        together = min(4, per)

        def some(k, c):
            for u in range(together):
                i = k * together + u
                n = q * per + i
                total = None
                for s in range(slots):
                    term = held[n * slots + s].astype(jnp.float32) * coef_wide[ids[s, n]]
                    total = term if total is None else total + term
                eta_rows[i] = jnp.sum(total.T, axis=0, keepdims=True)
            return c

        lax.fori_loop(0, per // together, some, 0)
        eta_parts[0, q * per : (q + 1) * per, :] = jnp.concatenate(
            [eta_rows[i] for i in range(per)], axis=0
        )

    chips = n_feat // 2
    chip, core = lax.div(mf, 2), lax.rem(mf, 2)
    my_half = pl.ds(pl.multiple_of(core * (rows // 2), 8), rows // 2)

    def pair_copy():
        return pltpu.make_async_remote_copy(
            src_ref=eta_parts.at[0], dst_ref=eta_parts.at[1],
            send_sem=pair_send, recv_sem=pair_recv,
            device_id=(me, chip * 2 + 1 - core), device_id_type=MESH,
        )

    def chip_send(d, to_core):
        pltpu.make_async_remote_copy(
            src_ref=eta_chips.at[0, my_half], dst_ref=eta_chips.at[d, my_half],
            send_sem=eta_send, recv_sem=eta_recv,
            device_id=(me, lax.rem(chip + d, chips) * 2 + to_core), device_id_type=MESH,
        ).start()

    lane = lanes_of(rows)
    row = lax.broadcasted_iota(jnp.int32, (rows, TILE), 0)
    diagonal = lane == row
    for q in range(CHUNKS):
        eta_make(q)
    for copy in small[1:]:
        copy.wait()
    gap = jnp.zeros((1, HALF - rows), jnp.int32)
    perm_all[0] = jnp.concatenate(
        [perm_buf[...], gap] * 2 if rows < HALF else [perm_buf[...]] * 2, axis=1
    )

    held[count] = jnp.zeros((TILE, TILE), jnp.bfloat16)
    resid_rows[rows] = jnp.zeros((1, TILE), jnp.float32)
    weight_rows[rows] = jnp.zeros((1, TILE), jnp.float32)
    running[running.shape[0] - 1] = jnp.zeros(running.shape[1:], jnp.float32)
    table_buf[...] = jnp.zeros_like(table_buf)

    event_flag = event_buf[...].astype(jnp.float32)
    group_bf = group_buf[...].astype(jnp.float32).astype(jnp.bfloat16)
    place = lax.broadcasted_iota(jnp.int32, (n_tm, rows), 1).astype(jnp.float32)
    perm_row = perm_all[0].astype(jnp.float32)
    perm_col = jnp.sum(jnp.where(diagonal, perm_row, 0.0), axis=1, keepdims=True)
    my_shard = jnp.floor(perm_col * (1.0 / rows))
    same = jnp.logical_and(jnp.floor(perm_row * (1.0 / rows)) == my_shard, perm_row < perm_col)
    rank = jnp.sum(
        jnp.where(jnp.logical_and(same, lane < rows), 1.0, 0.0), axis=1, keepdims=True
    )
    id_all = id_buf[...]
    block_at = lax.broadcasted_iota(jnp.int32, (blocks, rows), 0)
    row_at = lax.broadcasted_iota(jnp.int32, (blocks, rows), 1)
    present = jnp.zeros((blocks, rows), jnp.float32)
    which = jnp.zeros((blocks, rows), jnp.float32)
    for s in range(slots):
        here = id_all[s : s + 1, :] == block_at
        present = present + jnp.where(here, 1.0, 0.0)
        which = which + jnp.where(here, (row_at * slots + s).astype(jnp.float32), 0.0)
    before_row = jnp.where(
        lax.broadcasted_iota(jnp.int32, (rows, rows), 0)
        < lax.broadcasted_iota(jnp.int32, (rows, rows), 1), 1.0, 0.0,
    ).astype(jnp.bfloat16)
    rank_in = jnp.dot(present.astype(jnp.bfloat16), before_row, preferred_element_type=jnp.float32)
    rank_in = jnp.where(present > 0.5, rank_in, -1.0)
    number = jnp.sum(present, axis=1, keepdims=True)
    twos = jnp.floor((number + 1.0) * 0.5)
    square_row = lax.broadcasted_iota(jnp.int32, (blocks, blocks), 0)
    square_col = lax.broadcasted_iota(jnp.int32, (blocks, blocks), 1)
    number_row = jnp.sum(jnp.where(square_row == square_col, number, 0.0), axis=0, keepdims=True)
    twos_row = jnp.sum(jnp.where(square_row == square_col, twos, 0.0), axis=0, keepdims=True)
    start_row = jnp.sum(jnp.where(square_row < square_col, twos, 0.0), axis=0, keepdims=True)
    spot_row = lax.broadcasted_iota(jnp.int32, (TILE, TILE), 0)
    spot_col = lanes_of(TILE)
    for part in range(3):
        spot = (lax.broadcasted_iota(jnp.int32, (TILE, blocks), 0) + part * TILE).astype(jnp.float32)
        offset = spot - 2.0 * start_row
        inside = jnp.logical_and(offset >= 0.0, offset < number_row)
        member = jnp.where(inside, 1.0, 0.0).astype(jnp.bfloat16)
        wanted = jnp.sum(jnp.where(inside, offset, 0.0), axis=1, keepdims=True)
        filled = jnp.sum(jnp.where(inside, 1.0, 0.0), axis=1, keepdims=True)
        ranks = jnp.dot(member, rank_in.astype(jnp.bfloat16), preferred_element_type=jnp.float32)
        names = jnp.dot(member, which.astype(jnp.bfloat16), preferred_element_type=jnp.float32)
        chosen = jnp.sum(jnp.where(ranks == wanted, names, 0.0), axis=1, keepdims=True)
        chosen = jnp.where(filled > 0.5, jnp.minimum(chosen, 1.0 * count), 1.0 * count)
        for place_in, column in ((part, chosen), (3 + part, wanted)):
            table_buf[place_in : place_in + 1, :] = jnp.sum(
                jnp.where(spot_row == spot_col, column, 0.0), axis=0, keepdims=True
            ).astype(jnp.int32)
    empty = 1.0 * (running.shape[0] - 1)
    last_row = jnp.where(
        number_row > 0.5, jnp.minimum(start_row + twos_row - 1.0, empty), empty
    )
    table_buf[6:7, 0:blocks] = last_row.astype(jnp.int32)
    table_copy = pltpu.make_async_copy(table_buf, table, table_sem)
    table_copy.start()

    pl.semaphore_wait(barrier, n_tm + n_feat - 2)
    pair_copy().start()
    perm_how = (lambda i: perm_all.at[0], perm_all, perm_send, perm_recv, 1)
    tm_send(*perm_how)

    pair_copy().wait_recv()
    eta_chips[0] = eta_parts[0] + eta_parts[1]
    for d in sorted(range(1, chips), key=lambda d: -min(d, chips - d)):
        chip_send(d, 0)
        chip_send(d, 1)
    pair_copy().wait_send()
    if chips > 1:
        eta_all = all_of(eta_chips, eta_send, eta_recv, chips)
        eta_all.wait_recv()
        eta_all.wait_send()
    eta = eta_chips[lax.rem(chip, chips)]
    for c in range(1, chips):
        eta = eta + eta_chips[lax.rem(chip + chips - c, chips)]
    risk = jnp.exp(eta)
    sum_one[0] = jnp.sum(
        jnp.where(diagonal, jnp.sum(risk, axis=1, keepdims=True), 0.0), axis=0, keepdims=True
    )
    one_how = (lambda i: sum_one.at[0], sum_one, one_send, one_recv, 1)
    tm_send(*one_how)

    tm_wait(*perm_how)
    every = perm_all[:, 0, :].astype(jnp.float32)
    shard = jnp.floor(every * (1.0 / rows))
    within = every - shard * rows
    mine = jnp.logical_and(shard == me.astype(jnp.float32), lanes_of(n_tm) < rows)
    low = jnp.min(jnp.where(mine, within, 4096.0), axis=1, keepdims=True)
    high = jnp.max(jnp.where(mine, within, -1.0), axis=1, keepdims=True)
    group_low = jnp.dot(
        jnp.where(place == low, 1.0, 0.0).astype(jnp.bfloat16), group_bf,
        preferred_element_type=jnp.float32,
    )
    group_high = jnp.dot(
        jnp.where(place == high, 1.0, 0.0).astype(jnp.bfloat16), group_bf,
        preferred_element_type=jnp.float32,
    )
    for c in range(n_tm):
        group_send[c, :, 0:TILE] = group_low[c : c + 1, :]
        group_send[c, :, TILE : 2 * TILE] = group_high[c : c + 1, :]
    group_recv[0] = group_send[0]
    group_how = (lambda i: group_send.at[i], group_recv, grp_send, grp_recv, -1)
    tm_send(*group_how)

    source = lax.broadcasted_iota(jnp.int32, (TILE, TILE), 0)
    target = lanes_of(TILE)
    suffix = times_ones(risk, source >= target)
    tm_wait(*one_how)

    def add_later(c, total):
        return total + jnp.where(perm_all[c].astype(jnp.float32) > perm_col, sum_one[c], 0.0)

    after = lax.fori_loop(0, n_tm, add_later, jnp.zeros((rows, TILE), jnp.float32))
    after = jnp.sum(after, axis=1, keepdims=True)
    tm_wait(*group_how)
    shard_lane = lax.broadcasted_iota(jnp.int32, (rows, n_tm), 1).astype(jnp.float32)
    apart = my_shard - me.astype(jnp.float32)
    hit = jnp.where(shard_lane == apart + jnp.where(apart < 0.0, 1.0 * n_tm, 0.0), 1.0, 0.0)
    cohort_groups = jnp.dot(
        (hit * (1.0 - rank)).astype(jnp.bfloat16),
        group_recv[:, 0, 0:TILE].astype(jnp.bfloat16),
        preferred_element_type=jnp.float32,
    ) + jnp.dot(
        (hit * rank).astype(jnp.bfloat16),
        group_recv[:, 0, TILE : 2 * TILE].astype(jnp.bfloat16),
        preferred_element_type=jnp.float32,
    )
    later = suffix
    for k, d in enumerate(SHIFTS):
        back = pltpu.roll(cohort_groups, d, 1)
        tied = jnp.logical_and(lane >= d, back == cohort_groups)
        later = jnp.where(tied, pltpu.roll(later, d, 1), later)
    risk_total = later + after
    hazard_one = event_flag / risk_total
    hazard_two = hazard_one / risk_total
    sum_two[0] = jnp.sum(
        jnp.where(diagonal, jnp.sum(hazard_one, axis=1, keepdims=True), 0.0)
        + jnp.where(lane == row + HALF, jnp.sum(hazard_two, axis=1, keepdims=True), 0.0),
        axis=0, keepdims=True,
    )
    two_how = (lambda i: sum_two.at[0], sum_two, two_send, two_recv, 1)
    tm_send(*two_how)
    early_one = times_ones(hazard_one, source <= target)
    early_two = times_ones(hazard_two, source <= target)
    for k, d in enumerate(SHIFTS):
        ahead = pltpu.roll(cohort_groups, TILE - d, 1)
        tied = jnp.logical_and(lane < TILE - d, ahead == cohort_groups)
        early_one = jnp.where(tied, pltpu.roll(early_one, TILE - d, 1), early_one)
        early_two = jnp.where(tied, pltpu.roll(early_two, TILE - d, 1), early_two)
    tm_wait(*two_how)

    def add_early(c, total):
        return total + jnp.where(perm_all[c].astype(jnp.float32) < perm_col, sum_two[c], 0.0)

    before = lax.fori_loop(0, n_tm, add_early, jnp.zeros((rows, TILE), jnp.float32))
    cum_one = early_one + jnp.sum(
        jnp.where(lane < HALF, before, 0.0), axis=1, keepdims=True
    )
    cum_two = early_two + jnp.sum(
        jnp.where(lane < HALF, 0.0, before), axis=1, keepdims=True
    )
    resid = event_flag - risk * cum_one
    weight = risk * cum_one - risk * risk * cum_two
    for n in range(rows):
        resid_rows[n] = resid[n : n + 1, :]
        weight_rows[n] = weight[n : n + 1, :]

    table_copy.wait()
    steps = running.shape[0] - 1

    def gram_some(it, total):
        for u in range(UNROLL):
            m = it * UNROLL + u
            left, right = [], []
            for e in range(2):
                spot = 2 * m + e
                tile_at = table[lax.div(spot, TILE), lax.rem(spot, TILE)]
                tile_at = jnp.minimum(jnp.maximum(tile_at, 0), count)
                n = lax.div(tile_at, slots)
                tile = held[tile_at]
                turned = (tile.T.astype(jnp.float32) * weight_rows[n]).astype(jnp.bfloat16)
                rounded = jnp.broadcast_to(resid_rows[n], (16, TILE)).astype(jnp.bfloat16)
                left.append(jnp.concatenate([turned, rounded], axis=0))
                right.append(tile)
            keep = jnp.where(table[3 + lax.div(2 * m, TILE), lax.rem(2 * m, TILE)] > 0, 1.0, 0.0)
            total = total * keep + jnp.dot(
                jnp.concatenate(left, axis=1), jnp.concatenate(right, axis=0),
                preferred_element_type=jnp.float32,
            )
            running[m] = total
        return total

    lax.fori_loop(0, steps // UNROLL, gram_some, jnp.zeros((TILE + 16, TILE), jnp.float32))

    lane8 = lanes_of(8)
    sub8 = lax.broadcasted_iota(jnp.int32, (8, TILE), 0)

    def pack(block, to):
        at = jnp.minimum(jnp.maximum(table[6, block], 0), steps)
        whole = running[at, 0:TILE, :]
        whole = 0.5 * (whole + whole.T)
        for i in range(7):
            width = 120 - 8 * i
            low = whole[8 * (14 - i) : 8 * (14 - i) + 8, :]
            high = pltpu.roll(whole[8 * i : 8 * i + 8, :], width, 1)
            to[8 * i : 8 * i + 8, :] = jnp.where(lane8 < width, low, high)
        grad = running[at, TILE : TILE + 8, :]
        tail = jnp.where(sub8 == 0, grad, pltpu.roll(grad, HALF, 1))
        to[56:64, :] = jnp.where(lane8 < HALF, whole[56:64, :], tail)
        to[64:72, :] = whole[120:128, :]

    half_z = n_z // 2

    def far(k):
        return half_z + jnp.where(lax.rem(k, 2) == 1, -lax.div(k + 1, 2), lax.div(k, 2))

    def pack_for(k, dy):
        pack(lax.rem(z + far(k), n_z) * n_y + lax.rem(y + dy, n_y), packed.at[k, dy])

    half_rows = (pl.ds(0, CUT), pl.ds(CUT, PACK - CUT))
    ways = (1, n_y - 1)

    def chain_copy(k, w):
        return pltpu.make_async_remote_copy(
            src_ref=packed.at[k, 2, half_rows[w]], dst_ref=chain.at[k, half_rows[w]],
            send_sem=chain_send.at[w], recv_sem=chain_recv.at[w, k],
            device_id=(z * n_y + lax.rem(y + ways[w], n_y), mf), device_id_type=MESH,
        )

    def ring_copy(k, w):
        return pltpu.make_async_remote_copy(
            src_ref=packed.at[k, ways[w]], dst_ref=ring.at[w, k],
            send_sem=ring_send.at[w], recv_sem=ring_recv.at[w, k],
            device_id=(z * n_y + lax.rem(y + ways[w], n_y), mf), device_id_type=MESH,
        )

    def second_copy(k):
        return pltpu.make_async_remote_copy(
            src_ref=middle.at[k], dst_ref=second.at[k],
            send_sem=second_send, recv_sem=second_recv,
            device_id=(lax.rem(z + far(k), n_z) * n_y + y, mf), device_id_type=MESH,
        )

    def send_chain(k, c):
        pack_for(k, 2)
        for w in range(2):
            chain_copy(k, w).start()
        return c

    def send_ring(k, c):
        pack_for(k, 1)
        pack_for(k, 3)
        for w in range(2):
            chain_copy(k, w).wait_recv()
            packed[k, ways[w], half_rows[w], :] += chain[k, half_rows[w], :]
            ring_copy(k, w).start()
        return c

    def pack_own(k, c):
        pack_for(k, 0)
        return c

    def gathered(k):
        for w in range(2):
            ring_copy(k, w).wait_recv()
        return packed[k, 0] + ring[0, k] + ring[1, k]

    def send_second(k, c):
        middle[k] = gathered(k)
        second_copy(k).start()
        return c

    lax.fori_loop(0, n_z, send_chain, 0)
    lax.fori_loop(0, n_z, send_ring, 0)
    lax.fori_loop(0, n_z, pack_own, 0)
    lax.fori_loop(0, n_z - 1, send_second, 0)
    total = gathered(n_z - 1)
    second_all = all_of(second, second_send, second_recv, n_z)
    second_all.wait_recv()
    for k in range(n_z - 1):
        total = total + second[k]

    pieces = [total[8 * i : 8 * i + 8, :] for i in range(9)]
    turned = pltpu.roll(pieces[7], HALF, 1)
    gradient = jnp.where(lane8[0:1] < HALF, turned[1:2, :], pieces[7][0:1, :])
    grad_row[...] = gradient
    own_grad = pltpu.make_async_copy(grad_row, grad_out.at[me], own_sem.at[0])
    own_grad.start()

    def send_block(source, target, send_sem, recv_sem):
        def one(k, c):
            peer = lax.rem(me + outward(k, n_tm), n_tm)
            pltpu.make_async_remote_copy(
                src_ref=source, dst_ref=target.at[me], send_sem=send_sem, recv_sem=recv_sem,
                device_id=(peer, mf), device_id_type=MESH,
            ).start()
            return c

        lax.fori_loop(0, n_tm - 1, one, 0)

    send_block(grad_row, grad_out, grad_send, grad_recv)

    tile_rows = [pltpu.roll(pieces[i], 8 + 8 * i, 1) for i in range(7)]
    tile_rows += [pieces[7]] + [pieces[14 - i] for i in range(8, 15)] + [pieces[8]]
    stacked = jnp.concatenate(tile_rows, axis=0)
    row = spot_row
    lane = spot_col
    lower = jnp.where(lane <= row, stacked, 0.0)
    upper = jnp.where(lane < row, stacked, 0.0).T
    system = lower + upper + jnp.where(lane == row, 1.0, 0.0)
    column = jnp.sum(jnp.where(lane == row, gradient, 0.0), axis=1, keepdims=True)
    solved = eliminate(system, jnp.broadcast_to(column, (TILE, TILE)))
    answer = jnp.sum(jnp.where(lane == row, solved, 0.0), axis=0, keepdims=True)
    step_row[...] = answer
    own_step = pltpu.make_async_copy(step_row, step_out.at[me], own_sem.at[1])
    own_step.start()

    send_block(step_row, step_out, step_send, step_recv)
    for w in range(2):
        for sent, send_sem, recv_sem in (
            (chain.at[pl.ds(0, n_z), half_rows[w]], chain_send.at[w], chain_recv.at[w, 0]),
            (ring.at[w], ring_send.at[w], ring_recv.at[w, 0]),
        ):
            pltpu.make_async_remote_copy(
                src_ref=sent, dst_ref=sent, send_sem=send_sem, recv_sem=recv_sem,
                device_id=(lax.rem(me + 1, n_tm), mf), device_id_type=MESH,
            ).wait_send()
    second_all.wait_send()
    own_grad.wait()
    own_step.wait()
    for target, send_sem, recv_sem in (
        (grad_out, grad_send, grad_recv), (step_out, step_send, step_recv),
    ):
        copy = all_of(target, send_sem, recv_sem, n_tm)
        copy.wait_recv()
        copy.wait_send()


def hand_over_kernel(grad_in, step_in, grad_out, step_out, sems):
    copies = [
        pltpu.make_async_copy(source, target, sems.at[k])
        for k, (source, target) in enumerate(((grad_in, grad_out), (step_in, step_out)))
    ]
    for copy in copies:
        copy.start()
    for copy in copies:
        copy.wait()


def local(tile_data, tile_ids, owner_perm, events, groups, coefficients):
    rows, slots = tile_data.shape[:2]
    n_tm, n_feat = lax.axis_size("tm"), lax.axis_size("feat")
    n_y = Y_SIZE
    n_z = n_tm // n_y
    blocks = coefficients.shape[0] // TILE
    f32, vmem = jnp.float32, pl.BlockSpec(memory_space=pltpu.VMEM)
    smem, anywhere = pl.BlockSpec(memory_space=pltpu.SMEM), pl.BlockSpec(memory_space=pl.ANY)
    dma = pltpu.SemaphoreType.DMA
    ids = tile_ids.T
    count = rows * slots
    steps = -(-(count + blocks) // (2 * UNROLL)) * UNROLL

    gradient, step = pl.pallas_call(
        functools.partial(newton_kernel, n_z, n_y, n_feat),
        out_shape=[jax.ShapeDtypeStruct((n_tm, 1, TILE), f32)] * 2,
        in_specs=[anywhere, smem] + [anywhere] * 5,
        out_specs=[anywhere, anywhere],
        scratch_shapes=[
            pltpu.VMEM((count + 1, TILE, TILE), jnp.bfloat16),
            pltpu.VMEM((rows, TILE), jnp.int32),
            pltpu.VMEM((rows, TILE), jnp.int32),
            pltpu.VMEM((1, rows), jnp.int32),
            pltpu.VMEM((slots, rows), jnp.int32),
            pltpu.VMEM((blocks, TILE), jnp.bfloat16),
            pltpu.VMEM((blocks, 1, TILE), f32),
            pltpu.VMEM((rows // CHUNKS, 1, TILE), f32),
            pltpu.VMEM((2, rows, TILE), f32),
            pltpu.VMEM((n_feat // 2, rows, TILE), f32),
            pltpu.VMEM((n_tm, 1, TILE), jnp.int32),
            pltpu.VMEM((n_tm, 1, 2 * TILE), f32),
            pltpu.VMEM((n_tm, 1, 2 * TILE), f32),
            pltpu.VMEM((n_tm, 1, TILE), f32),
            pltpu.VMEM((n_tm, 1, TILE), f32),
            pltpu.VMEM((8, TILE), jnp.int32),
            pltpu.SMEM((8, TILE), jnp.int32),
            pltpu.VMEM((rows + 1, 1, TILE), f32),
            pltpu.VMEM((rows + 1, 1, TILE), f32),
            pltpu.VMEM((steps + 1, TILE + 16, TILE), f32),
            pltpu.VMEM((n_z, n_y, PACK, TILE), f32),
            pltpu.VMEM((n_z, PACK, TILE), f32),
            pltpu.VMEM((2, n_z, PACK, TILE), f32),
            pltpu.VMEM((n_z, PACK, TILE), f32),
            pltpu.VMEM((n_z, PACK, TILE), f32),
            pltpu.VMEM((1, TILE), f32),
            pltpu.VMEM((1, TILE), f32),
            dma((CHUNKS,)), dma((5,)), dma,
            dma, dma, dma, dma, dma, dma, dma, dma, dma, dma, dma, dma,
            dma((2,)), dma((2, n_z)), dma((2,)), dma((2, n_z)), dma, dma,
            dma, dma, dma, dma, dma((2,)),
        ],
        compiler_params=pltpu.CompilerParams(
            collective_id=0, has_side_effects=True, vmem_limit_bytes=60 * 2**20
        ),
        name="newton",
    )(
        tile_data.reshape(count, TILE, TILE), ids, ids, owner_perm.reshape(1, rows),
        events, groups, coefficients.reshape(blocks, TILE),
    )
    gradient, step = pl.pallas_call(
        hand_over_kernel,
        out_shape=[jax.ShapeDtypeStruct((n_tm, TILE), f32)] * 2,
        in_specs=[anywhere] * 2,
        out_specs=[anywhere] * 2,
        scratch_shapes=[dma((2,))],
        compiler_params=pltpu.CompilerParams(vmem_limit_bytes=60 * 2**20),
        name="hand_over",
    )(gradient.reshape(n_tm, TILE), step.reshape(n_tm, TILE))
    return gradient.reshape(-1), step.reshape(-1)


def solution(mesh):
    return jax.shard_map(
        local,
        mesh=mesh,
        in_specs=(
            P("tm", "feat", None, None),
            P("tm", "feat"),
            P("tm"),
            P("tm", None),
            P("tm", None),
            P("feat"),
        ),
        out_specs=(P("feat"), P("feat")),
        check_vma=False,
    )
```

```python
import functools

import jax
import jax.numpy as jnp
from jax import lax
from jax.experimental import pallas as pl
from jax.experimental.pallas import tpu as pltpu
from jax.sharding import PartitionSpec as P

MESH = pl.DeviceIdType.MESH
TILE = 128
HALF = 64
PACK = 72
SHIFTS = (1, 2, 4, 8, 16, 32, 64)
Y_SIZE = 4
CHUNKS = 4
CUT = 40
UNROLL = 36


def lanes_of(rows):
    return lax.broadcasted_iota(jnp.int32, (rows, TILE), 1)


def three_parts(x):
    high = x.astype(jnp.bfloat16)
    rest = x - high.astype(jnp.float32)
    mid = rest.astype(jnp.bfloat16)
    low = (rest - mid.astype(jnp.float32)).astype(jnp.bfloat16)
    return high, mid, low


def times_ones(x, mask):
    rows = x.shape[0]
    out = jnp.dot(
        jnp.concatenate(three_parts(x), axis=0),
        jnp.where(mask, 1.0, 0.0).astype(jnp.bfloat16),
        preferred_element_type=jnp.float32,
    )
    return out[2 * rows :] + out[rows : 2 * rows] + out[:rows]


def eliminate(system, rhs, wide=32):
    tiles = wide // 8
    sub = lax.broadcasted_iota(jnp.int32, (8, TILE), 0)

    def spread(x, r):
        return jnp.broadcast_to(x[r : r + 1, :], (8, TILE))

    def panel(p, carry):
        whole, right = carry
        a = [whole[8 * i : 8 * i + 8, :] for i in range(tiles)]
        g = [right[8 * i : 8 * i + 8, :] for i in range(tiles)]
        for q in range(tiles):
            cols = [
                [
                    jnp.broadcast_to(a[i][:, 8 * q + r : 8 * q + r + 1], (8, TILE))
                    for i in range(tiles)
                ]
                for r in range(8)
            ]
            head = [cols[r][q] for r in range(8)]
            top, top_g = a[q], g[q]
            for r in range(8):
                inverse = 1.0 / spread(head[r], r)
                factor = jnp.where(sub == r, inverse, -(head[r] * inverse))

                def step(x, r=r, factor=factor):
                    return jnp.where(sub == r, 0.0, x) + factor * spread(x, r)

                for k in range(r + 1, 8):
                    head[k] = step(head[k])
                top, top_g = step(top), step(top_g)
            for i in range(tiles):
                if i != q:
                    for r in range(8):
                        a[i] = a[i] - cols[r][i] * spread(top, r)
                        g[i] = g[i] - cols[r][i] * spread(top_g, r)
            a[q], g[q] = top, top_g
        done, done_g = jnp.concatenate(a, axis=0), jnp.concatenate(g, axis=0)
        rest = whole[wide:, :]
        update = jnp.dot(
            rest[:, :wide], jnp.concatenate([done, done_g], axis=1),
            precision=lax.Precision.HIGHEST, preferred_element_type=jnp.float32,
        )
        whole = jnp.concatenate([rest - update[:, :TILE], done], axis=0)
        right = jnp.concatenate([right[wide:, :] - update[:, TILE:], done_g], axis=0)
        return pltpu.roll(whole, TILE - wide, 1), right

    return lax.fori_loop(0, TILE // wide, panel, (system, rhs))[1]


def newton_kernel(
    n_z, n_y, n_feat,
    tiles, ids, id_rows, perm, events, groups, coef,
    grad_out, step_out,
    held, event_buf, group_buf, perm_buf, id_buf, coef_buf, coef_wide, eta_rows,
    eta_parts, eta_chips, perm_all, group_send, group_recv, sum_one, sum_two,
    table_buf, table, weight_rows, resid_rows, running,
    packed, chain, ring, middle, second, grad_row, step_row,
    tile_sem, small_sem, table_sem, pair_send, pair_recv, eta_send, eta_recv, perm_send, perm_recv, grp_send, grp_recv,
    one_send, one_recv, two_send, two_recv,
    chain_send, chain_recv, ring_send, ring_recv, second_send, second_recv,
    grad_send, grad_recv, step_send, step_recv, own_sem,
):
    n_tm = n_z * n_y
    z = lax.div(lax.axis_index("tm"), n_y)
    y = lax.rem(lax.axis_index("tm"), n_y)
    me = lax.axis_index("tm")
    mf = lax.axis_index("feat")
    rows = events.shape[0]
    per = rows // CHUNKS
    slots, blocks = id_rows.shape[0], coef.shape[0]
    count = rows * slots
    barrier = pltpu.get_barrier_semaphore()

    def outward(k, size):
        return size // 2 + jnp.where(lax.rem(k, 2) == 1, -lax.div(k + 1, 2), lax.div(k, 2))

    def greet_tm(k, c):
        peer = lax.rem(me + outward(k, n_tm), n_tm)
        pl.semaphore_signal(barrier, inc=1, device_id=(peer, mf), device_id_type=MESH)
        return c

    def greet_feat(k, c):
        peer = lax.rem(mf + outward(k, n_feat), n_feat)
        pl.semaphore_signal(barrier, inc=1, device_id=(me, peer), device_id_type=MESH)
        return c

    def tile_copy(q):
        part = pl.ds(q * per * slots, per * slots)
        return pltpu.make_async_copy(tiles.at[part], held.at[part], tile_sem.at[q])

    small = [
        pltpu.make_async_copy(source, target, small_sem.at[k])
        for k, (source, target) in enumerate(
            ((coef, coef_buf), (perm, perm_buf), (groups, group_buf), (events, event_buf), (id_rows, id_buf))
        )
    ]
    lax.fori_loop(0, n_tm - 1, greet_tm, 0)
    lax.fori_loop(0, n_feat - 1, greet_feat, 0)
    small[0].start()
    for q in range(CHUNKS):
        tile_copy(q).start()
    for copy in small[1:]:
        copy.start()

    def tm_send(source, target, send_sem, recv_sem, sign):
        def one(k, c):
            i = outward(k, n_tm)
            pltpu.make_async_remote_copy(
                src_ref=source(i), dst_ref=target.at[i], send_sem=send_sem, recv_sem=recv_sem,
                device_id=(lax.rem(me + sign * i + n_tm, n_tm), mf), device_id_type=MESH,
            ).start()
            return c

        lax.fori_loop(0, n_tm - 1, one, 0)

    def all_of(target, send_sem, recv_sem, size):
        places = target.at[pl.ds(1, size - 1)]
        return pltpu.make_async_remote_copy(
            src_ref=places, dst_ref=places, send_sem=send_sem, recv_sem=recv_sem,
            device_id=(lax.rem(me + 1, n_tm), mf), device_id_type=MESH,
        )

    def tm_wait(source, target, send_sem, recv_sem, sign):
        copy = all_of(target, send_sem, recv_sem, n_tm)
        copy.wait_recv()
        copy.wait_send()

    small[0].wait()
    wide = coef_buf[...].astype(jnp.float32)
    for j in range(blocks):
        coef_wide[j] = wide[j : j + 1, :]

    def eta_make(q):
        tile_copy(q).wait()
        together = min(4, per)

        def some(k, c):
            for u in range(together):
                i = k * together + u
                n = q * per + i
                total = None
                for s in range(slots):
                    term = held[n * slots + s].astype(jnp.float32) * coef_wide[ids[s, n]]
                    total = term if total is None else total + term
                eta_rows[i] = jnp.sum(total.T, axis=0, keepdims=True)
            return c

        lax.fori_loop(0, per // together, some, 0)
        eta_parts[0, q * per : (q + 1) * per, :] = jnp.concatenate(
            [eta_rows[i] for i in range(per)], axis=0
        )

    chips = n_feat // 2
    chip, core = lax.div(mf, 2), lax.rem(mf, 2)
    my_half = pl.ds(pl.multiple_of(core * (rows // 2), 8), rows // 2)

    def pair_copy():
        return pltpu.make_async_remote_copy(
            src_ref=eta_parts.at[0], dst_ref=eta_parts.at[1],
            send_sem=pair_send, recv_sem=pair_recv,
            device_id=(me, chip * 2 + 1 - core), device_id_type=MESH,
        )

    def chip_send(d, to_core):
        pltpu.make_async_remote_copy(
            src_ref=eta_chips.at[0, my_half], dst_ref=eta_chips.at[d, my_half],
            send_sem=eta_send, recv_sem=eta_recv,
            device_id=(me, lax.rem(chip + d, chips) * 2 + to_core), device_id_type=MESH,
        ).start()

    lane = lanes_of(rows)
    row = lax.broadcasted_iota(jnp.int32, (rows, TILE), 0)
    diagonal = lane == row
    for q in range(CHUNKS):
        eta_make(q)
    for copy in small[1:]:
        copy.wait()
    gap = jnp.zeros((1, HALF - rows), jnp.int32)
    perm_all[0] = jnp.concatenate(
        [perm_buf[...], gap] * 2 if rows < HALF else [perm_buf[...]] * 2, axis=1
    )

    held[count] = jnp.zeros((TILE, TILE), jnp.bfloat16)
    resid_rows[rows] = jnp.zeros((1, TILE), jnp.float32)
    weight_rows[rows] = jnp.zeros((1, TILE), jnp.float32)
    running[running.shape[0] - 1] = jnp.zeros(running.shape[1:], jnp.float32)
    table_buf[...] = jnp.zeros_like(table_buf)

    event_flag = event_buf[...].astype(jnp.float32)
    group_bf = group_buf[...].astype(jnp.float32).astype(jnp.bfloat16)
    place = lax.broadcasted_iota(jnp.int32, (n_tm, rows), 1).astype(jnp.float32)
    perm_row = perm_all[0].astype(jnp.float32)
    perm_col = jnp.sum(jnp.where(diagonal, perm_row, 0.0), axis=1, keepdims=True)
    my_shard = jnp.floor(perm_col * (1.0 / rows))
    same = jnp.logical_and(jnp.floor(perm_row * (1.0 / rows)) == my_shard, perm_row < perm_col)
    rank = jnp.sum(
        jnp.where(jnp.logical_and(same, lane < rows), 1.0, 0.0), axis=1, keepdims=True
    )
    id_all = id_buf[...]
    block_at = lax.broadcasted_iota(jnp.int32, (blocks, rows), 0)
    row_at = lax.broadcasted_iota(jnp.int32, (blocks, rows), 1)
    present = jnp.zeros((blocks, rows), jnp.float32)
    which = jnp.zeros((blocks, rows), jnp.float32)
    for s in range(slots):
        here = id_all[s : s + 1, :] == block_at
        present = present + jnp.where(here, 1.0, 0.0)
        which = which + jnp.where(here, (row_at * slots + s).astype(jnp.float32), 0.0)
    before_row = jnp.where(
        lax.broadcasted_iota(jnp.int32, (rows, rows), 0)
        < lax.broadcasted_iota(jnp.int32, (rows, rows), 1), 1.0, 0.0,
    ).astype(jnp.bfloat16)
    rank_in = jnp.dot(present.astype(jnp.bfloat16), before_row, preferred_element_type=jnp.float32)
    rank_in = jnp.where(present > 0.5, rank_in, -1.0)
    number = jnp.sum(present, axis=1, keepdims=True)
    twos = jnp.floor((number + 1.0) * 0.5)
    square_row = lax.broadcasted_iota(jnp.int32, (blocks, blocks), 0)
    square_col = lax.broadcasted_iota(jnp.int32, (blocks, blocks), 1)
    number_row = jnp.sum(jnp.where(square_row == square_col, number, 0.0), axis=0, keepdims=True)
    twos_row = jnp.sum(jnp.where(square_row == square_col, twos, 0.0), axis=0, keepdims=True)
    start_row = jnp.sum(jnp.where(square_row < square_col, twos, 0.0), axis=0, keepdims=True)
    spot_row = lax.broadcasted_iota(jnp.int32, (TILE, TILE), 0)
    spot_col = lanes_of(TILE)
    for part in range(3):
        spot = (lax.broadcasted_iota(jnp.int32, (TILE, blocks), 0) + part * TILE).astype(jnp.float32)
        offset = spot - 2.0 * start_row
        inside = jnp.logical_and(offset >= 0.0, offset < number_row)
        member = jnp.where(inside, 1.0, 0.0).astype(jnp.bfloat16)
        wanted = jnp.sum(jnp.where(inside, offset, 0.0), axis=1, keepdims=True)
        filled = jnp.sum(jnp.where(inside, 1.0, 0.0), axis=1, keepdims=True)
        ranks = jnp.dot(member, rank_in.astype(jnp.bfloat16), preferred_element_type=jnp.float32)
        names = jnp.dot(member, which.astype(jnp.bfloat16), preferred_element_type=jnp.float32)
        chosen = jnp.sum(jnp.where(ranks == wanted, names, 0.0), axis=1, keepdims=True)
        chosen = jnp.where(filled > 0.5, jnp.minimum(chosen, 1.0 * count), 1.0 * count)
        for place_in, column in ((part, chosen), (3 + part, wanted)):
            table_buf[place_in : place_in + 1, :] = jnp.sum(
                jnp.where(spot_row == spot_col, column, 0.0), axis=0, keepdims=True
            ).astype(jnp.int32)
    empty = 1.0 * (running.shape[0] - 1)
    last_row = jnp.where(
        number_row > 0.5, jnp.minimum(start_row + twos_row - 1.0, empty), empty
    )
    table_buf[6:7, 0:blocks] = last_row.astype(jnp.int32)
    table_copy = pltpu.make_async_copy(table_buf, table, table_sem)
    table_copy.start()

    pl.semaphore_wait(barrier, n_tm + n_feat - 2)
    pair_copy().start()
    perm_how = (lambda i: perm_all.at[0], perm_all, perm_send, perm_recv, 1)
    tm_send(*perm_how)

    pair_copy().wait_recv()
    eta_chips[0] = eta_parts[0] + eta_parts[1]
    for d in sorted(range(1, chips), key=lambda d: -min(d, chips - d)):
        chip_send(d, 0)
        chip_send(d, 1)
    pair_copy().wait_send()
    if chips > 1:
        eta_all = all_of(eta_chips, eta_send, eta_recv, chips)
        eta_all.wait_recv()
        eta_all.wait_send()
    eta = eta_chips[lax.rem(chip, chips)]
    for c in range(1, chips):
        eta = eta + eta_chips[lax.rem(chip + chips - c, chips)]
    risk = jnp.exp(eta)
    sum_one[0] = jnp.sum(
        jnp.where(diagonal, jnp.sum(risk, axis=1, keepdims=True), 0.0), axis=0, keepdims=True
    )
    one_how = (lambda i: sum_one.at[0], sum_one, one_send, one_recv, 1)
    tm_send(*one_how)

    tm_wait(*perm_how)
    every = perm_all[:, 0, :].astype(jnp.float32)
    shard = jnp.floor(every * (1.0 / rows))
    within = every - shard * rows
    mine = jnp.logical_and(shard == me.astype(jnp.float32), lanes_of(n_tm) < rows)
    low = jnp.min(jnp.where(mine, within, 4096.0), axis=1, keepdims=True)
    high = jnp.max(jnp.where(mine, within, -1.0), axis=1, keepdims=True)
    group_low = jnp.dot(
        jnp.where(place == low, 1.0, 0.0).astype(jnp.bfloat16), group_bf,
        preferred_element_type=jnp.float32,
    )
    group_high = jnp.dot(
        jnp.where(place == high, 1.0, 0.0).astype(jnp.bfloat16), group_bf,
        preferred_element_type=jnp.float32,
    )
    for c in range(n_tm):
        group_send[c, :, 0:TILE] = group_low[c : c + 1, :]
        group_send[c, :, TILE : 2 * TILE] = group_high[c : c + 1, :]
    group_recv[0] = group_send[0]
    group_how = (lambda i: group_send.at[i], group_recv, grp_send, grp_recv, -1)
    tm_send(*group_how)

    source = lax.broadcasted_iota(jnp.int32, (TILE, TILE), 0)
    target = lanes_of(TILE)
    suffix = times_ones(risk, source >= target)
    tm_wait(*one_how)

    def add_later(c, total):
        return total + jnp.where(perm_all[c].astype(jnp.float32) > perm_col, sum_one[c], 0.0)

    after = lax.fori_loop(
        0, n_tm, add_later, jnp.zeros((rows, TILE), jnp.float32), unroll=8
    )
    after = jnp.sum(after, axis=1, keepdims=True)
    tm_wait(*group_how)
    shard_lane = lax.broadcasted_iota(jnp.int32, (rows, n_tm), 1).astype(jnp.float32)
    apart = my_shard - me.astype(jnp.float32)
    hit = jnp.where(shard_lane == apart + jnp.where(apart < 0.0, 1.0 * n_tm, 0.0), 1.0, 0.0)
    cohort_groups = jnp.dot(
        (hit * (1.0 - rank)).astype(jnp.bfloat16),
        group_recv[:, 0, 0:TILE].astype(jnp.bfloat16),
        preferred_element_type=jnp.float32,
    ) + jnp.dot(
        (hit * rank).astype(jnp.bfloat16),
        group_recv[:, 0, TILE : 2 * TILE].astype(jnp.bfloat16),
        preferred_element_type=jnp.float32,
    )
    later = suffix
    for k, d in enumerate(SHIFTS):
        back = pltpu.roll(cohort_groups, d, 1)
        tied = jnp.logical_and(lane >= d, back == cohort_groups)
        later = jnp.where(tied, pltpu.roll(later, d, 1), later)
    risk_total = later + after
    hazard_one = event_flag / risk_total
    hazard_two = hazard_one / risk_total
    sum_two[0] = jnp.sum(
        jnp.where(diagonal, jnp.sum(hazard_one, axis=1, keepdims=True), 0.0)
        + jnp.where(lane == row + HALF, jnp.sum(hazard_two, axis=1, keepdims=True), 0.0),
        axis=0, keepdims=True,
    )
    two_how = (lambda i: sum_two.at[0], sum_two, two_send, two_recv, 1)
    tm_send(*two_how)
    early_one = times_ones(hazard_one, source <= target)
    early_two = times_ones(hazard_two, source <= target)
    for k, d in enumerate(SHIFTS):
        ahead = pltpu.roll(cohort_groups, TILE - d, 1)
        tied = jnp.logical_and(lane < TILE - d, ahead == cohort_groups)
        early_one = jnp.where(tied, pltpu.roll(early_one, TILE - d, 1), early_one)
        early_two = jnp.where(tied, pltpu.roll(early_two, TILE - d, 1), early_two)
    tm_wait(*two_how)

    def add_early(c, total):
        return total + jnp.where(perm_all[c].astype(jnp.float32) < perm_col, sum_two[c], 0.0)

    before = lax.fori_loop(
        0, n_tm, add_early, jnp.zeros((rows, TILE), jnp.float32), unroll=8
    )
    cum_one = early_one + jnp.sum(
        jnp.where(lane < HALF, before, 0.0), axis=1, keepdims=True
    )
    cum_two = early_two + jnp.sum(
        jnp.where(lane < HALF, 0.0, before), axis=1, keepdims=True
    )
    resid = event_flag - risk * cum_one
    weight = risk * cum_one - risk * risk * cum_two
    for n in range(rows):
        resid_rows[n] = resid[n : n + 1, :]
        weight_rows[n] = weight[n : n + 1, :]

    table_copy.wait()
    steps = running.shape[0] - 1

    def gram_some(it, total):
        for u in range(UNROLL):
            m = it * UNROLL + u
            left, right = [], []
            for e in range(2):
                spot = 2 * m + e
                tile_at = table[lax.div(spot, TILE), lax.rem(spot, TILE)]
                tile_at = jnp.minimum(jnp.maximum(tile_at, 0), count)
                n = lax.div(tile_at, slots)
                tile = held[tile_at]
                turned = (tile.T.astype(jnp.float32) * weight_rows[n]).astype(jnp.bfloat16)
                rounded = jnp.broadcast_to(resid_rows[n], (16, TILE)).astype(jnp.bfloat16)
                left.append(jnp.concatenate([turned, rounded], axis=0))
                right.append(tile)
            keep = jnp.where(table[3 + lax.div(2 * m, TILE), lax.rem(2 * m, TILE)] > 0, 1.0, 0.0)
            total = total * keep + jnp.dot(
                jnp.concatenate(left, axis=1), jnp.concatenate(right, axis=0),
                preferred_element_type=jnp.float32,
            )
            running[m] = total
        return total

    lax.fori_loop(0, steps // UNROLL, gram_some, jnp.zeros((TILE + 16, TILE), jnp.float32))

    lane8 = lanes_of(8)
    sub8 = lax.broadcasted_iota(jnp.int32, (8, TILE), 0)

    def pack(block, to):
        at = jnp.minimum(jnp.maximum(table[6, block], 0), steps)
        whole = running[at, 0:TILE, :]
        whole = 0.5 * (whole + whole.T)
        for i in range(7):
            width = 120 - 8 * i
            low = whole[8 * (14 - i) : 8 * (14 - i) + 8, :]
            high = pltpu.roll(whole[8 * i : 8 * i + 8, :], width, 1)
            to[8 * i : 8 * i + 8, :] = jnp.where(lane8 < width, low, high)
        grad = running[at, TILE : TILE + 8, :]
        tail = jnp.where(sub8 == 0, grad, pltpu.roll(grad, HALF, 1))
        to[56:64, :] = jnp.where(lane8 < HALF, whole[56:64, :], tail)
        to[64:72, :] = whole[120:128, :]

    half_z = n_z // 2

    def far(k):
        return half_z + jnp.where(lax.rem(k, 2) == 1, -lax.div(k + 1, 2), lax.div(k, 2))

    def pack_for(k, dy):
        pack(lax.rem(z + far(k), n_z) * n_y + lax.rem(y + dy, n_y), packed.at[k, dy])

    half_rows = (pl.ds(0, CUT), pl.ds(CUT, PACK - CUT))
    ways = (1, n_y - 1)

    def chain_copy(k, w):
        return pltpu.make_async_remote_copy(
            src_ref=packed.at[k, 2, half_rows[w]], dst_ref=chain.at[k, half_rows[w]],
            send_sem=chain_send.at[w], recv_sem=chain_recv.at[w, k],
            device_id=(z * n_y + lax.rem(y + ways[w], n_y), mf), device_id_type=MESH,
        )

    def ring_copy(k, w):
        return pltpu.make_async_remote_copy(
            src_ref=packed.at[k, ways[w]], dst_ref=ring.at[w, k],
            send_sem=ring_send.at[w], recv_sem=ring_recv.at[w, k],
            device_id=(z * n_y + lax.rem(y + ways[w], n_y), mf), device_id_type=MESH,
        )

    def second_copy(k):
        return pltpu.make_async_remote_copy(
            src_ref=middle.at[k], dst_ref=second.at[k],
            send_sem=second_send, recv_sem=second_recv,
            device_id=(lax.rem(z + far(k), n_z) * n_y + y, mf), device_id_type=MESH,
        )

    def send_chain(k, c):
        pack_for(k, 2)
        for w in range(2):
            chain_copy(k, w).start()
        return c

    def send_ring(k, c):
        pack_for(k, 1)
        pack_for(k, 3)
        for w in range(2):
            chain_copy(k, w).wait_recv()
            packed[k, ways[w], half_rows[w], :] += chain[k, half_rows[w], :]
            ring_copy(k, w).start()
        return c

    def pack_own(k, c):
        pack_for(k, 0)
        return c

    def gathered(k):
        for w in range(2):
            ring_copy(k, w).wait_recv()
        return packed[k, 0] + ring[0, k] + ring[1, k]

    def send_second(k, c):
        middle[k] = gathered(k)
        second_copy(k).start()
        return c

    lax.fori_loop(0, n_z, send_chain, 0)
    lax.fori_loop(0, n_z, send_ring, 0)
    lax.fori_loop(0, n_z, pack_own, 0)
    lax.fori_loop(0, n_z - 1, send_second, 0)
    total = gathered(n_z - 1)
    second_all = all_of(second, second_send, second_recv, n_z)
    second_all.wait_recv()
    for k in range(n_z - 1):
        total = total + second[k]

    pieces = [total[8 * i : 8 * i + 8, :] for i in range(9)]
    turned = pltpu.roll(pieces[7], HALF, 1)
    gradient = jnp.where(lane8[0:1] < HALF, turned[1:2, :], pieces[7][0:1, :])
    grad_row[...] = gradient
    own_grad = pltpu.make_async_copy(grad_row, grad_out.at[me], own_sem.at[0])
    own_grad.start()

    def send_block(source, target, send_sem, recv_sem):
        def one(k, c):
            peer = lax.rem(me + outward(k, n_tm), n_tm)
            pltpu.make_async_remote_copy(
                src_ref=source, dst_ref=target.at[me], send_sem=send_sem, recv_sem=recv_sem,
                device_id=(peer, mf), device_id_type=MESH,
            ).start()
            return c

        lax.fori_loop(0, n_tm - 1, one, 0)

    send_block(grad_row, grad_out, grad_send, grad_recv)

    tile_rows = [pltpu.roll(pieces[i], 8 + 8 * i, 1) for i in range(7)]
    tile_rows += [pieces[7]] + [pieces[14 - i] for i in range(8, 15)] + [pieces[8]]
    stacked = jnp.concatenate(tile_rows, axis=0)
    row = spot_row
    lane = spot_col
    lower = jnp.where(lane <= row, stacked, 0.0)
    upper = jnp.where(lane < row, stacked, 0.0).T
    system = lower + upper + jnp.where(lane == row, 1.0, 0.0)
    column = jnp.sum(jnp.where(lane == row, gradient, 0.0), axis=1, keepdims=True)
    solved = eliminate(system, jnp.broadcast_to(column, (TILE, TILE)))
    answer = jnp.sum(jnp.where(lane == row, solved, 0.0), axis=0, keepdims=True)
    step_row[...] = answer
    own_step = pltpu.make_async_copy(step_row, step_out.at[me], own_sem.at[1])
    own_step.start()

    send_block(step_row, step_out, step_send, step_recv)
    for w in range(2):
        for sent, send_sem, recv_sem in (
            (chain.at[pl.ds(0, n_z), half_rows[w]], chain_send.at[w], chain_recv.at[w, 0]),
            (ring.at[w], ring_send.at[w], ring_recv.at[w, 0]),
        ):
            pltpu.make_async_remote_copy(
                src_ref=sent, dst_ref=sent, send_sem=send_sem, recv_sem=recv_sem,
                device_id=(lax.rem(me + 1, n_tm), mf), device_id_type=MESH,
            ).wait_send()
    second_all.wait_send()
    own_grad.wait()
    own_step.wait()
    for target, send_sem, recv_sem in (
        (grad_out, grad_send, grad_recv), (step_out, step_send, step_recv),
    ):
        copy = all_of(target, send_sem, recv_sem, n_tm)
        copy.wait_recv()
        copy.wait_send()


def hand_over_kernel(grad_in, step_in, grad_out, step_out, sems):
    copies = [
        pltpu.make_async_copy(source, target, sems.at[k])
        for k, (source, target) in enumerate(((grad_in, grad_out), (step_in, step_out)))
    ]
    for copy in copies:
        copy.start()
    for copy in copies:
        copy.wait()


def local(tile_data, tile_ids, owner_perm, events, groups, coefficients):
    rows, slots = tile_data.shape[:2]
    n_tm, n_feat = lax.axis_size("tm"), lax.axis_size("feat")
    n_y = Y_SIZE
    n_z = n_tm // n_y
    blocks = coefficients.shape[0] // TILE
    f32, vmem = jnp.float32, pl.BlockSpec(memory_space=pltpu.VMEM)
    smem, anywhere = pl.BlockSpec(memory_space=pltpu.SMEM), pl.BlockSpec(memory_space=pl.ANY)
    dma = pltpu.SemaphoreType.DMA
    ids = tile_ids.T
    count = rows * slots
    steps = -(-(count + blocks) // (2 * UNROLL)) * UNROLL

    gradient, step = pl.pallas_call(
        functools.partial(newton_kernel, n_z, n_y, n_feat),
        out_shape=[jax.ShapeDtypeStruct((n_tm, 1, TILE), f32)] * 2,
        in_specs=[anywhere, smem] + [anywhere] * 5,
        out_specs=[anywhere, anywhere],
        scratch_shapes=[
            pltpu.VMEM((count + 1, TILE, TILE), jnp.bfloat16),
            pltpu.VMEM((rows, TILE), jnp.int32),
            pltpu.VMEM((rows, TILE), jnp.int32),
            pltpu.VMEM((1, rows), jnp.int32),
            pltpu.VMEM((slots, rows), jnp.int32),
            pltpu.VMEM((blocks, TILE), jnp.bfloat16),
            pltpu.VMEM((blocks, 1, TILE), f32),
            pltpu.VMEM((rows // CHUNKS, 1, TILE), f32),
            pltpu.VMEM((2, rows, TILE), f32),
            pltpu.VMEM((n_feat // 2, rows, TILE), f32),
            pltpu.VMEM((n_tm, 1, TILE), jnp.int32),
            pltpu.VMEM((n_tm, 1, 2 * TILE), f32),
            pltpu.VMEM((n_tm, 1, 2 * TILE), f32),
            pltpu.VMEM((n_tm, 1, TILE), f32),
            pltpu.VMEM((n_tm, 1, TILE), f32),
            pltpu.VMEM((8, TILE), jnp.int32),
            pltpu.SMEM((8, TILE), jnp.int32),
            pltpu.VMEM((rows + 1, 1, TILE), f32),
            pltpu.VMEM((rows + 1, 1, TILE), f32),
            pltpu.VMEM((steps + 1, TILE + 16, TILE), f32),
            pltpu.VMEM((n_z, n_y, PACK, TILE), f32),
            pltpu.VMEM((n_z, PACK, TILE), f32),
            pltpu.VMEM((2, n_z, PACK, TILE), f32),
            pltpu.VMEM((n_z, PACK, TILE), f32),
            pltpu.VMEM((n_z, PACK, TILE), f32),
            pltpu.VMEM((1, TILE), f32),
            pltpu.VMEM((1, TILE), f32),
            dma((CHUNKS,)), dma((5,)), dma,
            dma, dma, dma, dma, dma, dma, dma, dma, dma, dma, dma, dma,
            dma((2,)), dma((2, n_z)), dma((2,)), dma((2, n_z)), dma, dma,
            dma, dma, dma, dma, dma((2,)),
        ],
        compiler_params=pltpu.CompilerParams(
            collective_id=0, has_side_effects=True, vmem_limit_bytes=60 * 2**20
        ),
        name="newton",
    )(
        tile_data.reshape(count, TILE, TILE), ids, ids, owner_perm.reshape(1, rows),
        events, groups, coefficients.reshape(blocks, TILE),
    )
    gradient, step = pl.pallas_call(
        hand_over_kernel,
        out_shape=[jax.ShapeDtypeStruct((n_tm, TILE), f32)] * 2,
        in_specs=[anywhere] * 2,
        out_specs=[anywhere] * 2,
        scratch_shapes=[dma((2,))],
        compiler_params=pltpu.CompilerParams(vmem_limit_bytes=60 * 2**20),
        name="hand_over",
    )(gradient.reshape(n_tm, TILE), step.reshape(n_tm, TILE))
    return gradient.reshape(-1), step.reshape(-1)


def solution(mesh):
    return jax.shard_map(
        local,
        mesh=mesh,
        in_specs=(
            P("tm", "feat", None, None),
            P("tm", "feat"),
            P("tm"),
            P("tm", None),
            P("tm", None),
            P("feat"),
        ),
        out_specs=(P("feat"), P("feat")),
        check_vma=False,
    )
```
